128 devices in a mesh: blk: 4 (over x_lo, core), tensor: 32 (over y, z, x_hi).
Axes of the slice: x: 4 (x_hi: 2, x_lo: 2; x = x_hi * 2 + x_lo), y: 4, z: 4, core: 2. Of those that a mesh axis runs over, the one named last changes fastest.
Arguments:
- tokens: bfloat16 [4096, 8192], P('tensor', 'blk'), may hold values from -6 to 6
- norm_gain: float32 [8192], P('blk'), may hold values from 0.1 to 1.9
- segment_ids: int32 [4096], replicated, may hold values from 0 to 15, never falling along the last dimension, each value on 1 to 2049 neighbouring positions
- w_query: bfloat16 [8192, 8192], P('blk', 'tensor'), may hold values from -0.0625 to 0.0625
- key_weight: bfloat16 [8192, 1024], P('blk'), may hold values from -0.0625 to 0.0625
- value_weight: bfloat16 [8192, 1024], P('blk'), may hold values from -0.0625 to 0.0625
- w_output: bfloat16 [8192, 8192], P('tensor', 'blk'), may hold values from -0.25 to 0.25
Outputs:
- block_out: bfloat16 [4096, 8192], P('tensor', 'blk')
The draws below stay inside these ranges and needn't reach their ends.
Inputs may be any that keep to these rules, and one draw needn't show every extreme that they name: `segment_ids`: segment ids never fall along the tokens; each rollout holds 1 to 2049 consecutive tokens and one holds exactly 2049.
All inputs are finite; a program needn't handle non-finite values.
Results may differ from the reference program's by a relative error of at most 0.04.
Values may be sent and summed in bfloat16 or wider, within the bound.
No kernel may reach another device: no remote copies, remote signals or barrier semaphores. Data moves between devices by JAX's collectives and lax.ppermute only.
A program may use at most 128 MiB of HBM per device.

```python
import math
import jax
import jax.numpy as jnp
import numpy as np
from jax import lax

MODEL_WIDTH = 8192
QUERY_HEADS = 64
KEY_VALUE_HEADS = 8
HEAD_SIZE = 128
TOKENS = 4096
N_TENSOR = 32


def level_of(key, dims, pieces, least, high):
    gain, own = 1.0, jax.random.fold_in(key, 6)
    for dim, parts in pieces:
        steps = jnp.exp(jax.random.uniform(jax.random.fold_in(own, dim), (parts,), jnp.float32, least / len(pieces), high / len(pieces)))
        gain = gain * jnp.repeat(steps, dims[dim] // parts).reshape([-1 if axis == dim else 1 for axis in range(len(dims))])
    return gain


def profile(count, total, bound, slope):
    loads = [(1 << 20) // math.isqrt(grade ** slope) + 1 for grade in range(2, count + 1)]
    rest, counts = total - bound - (count - 1), [1] * (count - 1)
    while rest > 0:
        candidates = [i for i in range(count - 1) if counts[i] < bound]
        mass, left = sum([loads[i] for i in candidates]), rest
        for i in candidates:
            extra = min(bound - counts[i], max(1, left * loads[i] // mass), rest)
            counts[i] = counts[i] + extra
            rest = rest - extra
    return np.array([bound] + counts)


def uneven_parts(key, amount, total, most, lean):
    if amount == 2:
        one = jax.random.randint(key, (), max(1, total - most), min(most, total - 1) + 1)
        return jnp.stack([one, total - one])
    tallies = jnp.asarray(profile(amount, total, most, lean), jnp.int32)
    couples = (amount - 1) // 2
    source_of, receiver = tallies[1:1 + 2 * couples:2], tallies[2:2 + 2 * couples:2]
    room = jnp.minimum(source_of - 1, most - receiver)
    shifted = jax.random.randint(jax.random.fold_in(key, 1), (couples,), 0, 1 << 20) % (room + 1)
    tallies = tallies.at[1:1 + 2 * couples:2].set(source_of - shifted).at[2:2 + 2 * couples:2].set(receiver + shifted)
    return tallies[jax.random.permutation(jax.random.fold_in(key, 2), amount)]


def noise(key, extent, spread, bound, shards=(), kind=jnp.bfloat16):
    factor_of = level_of(key, extent, shards, -0.22, 0.18) if shards else 1.0
    entries = jax.random.normal(key, extent, jnp.float32) * spread * factor_of
    return jnp.minimum(jnp.maximum(entries, -bound), bound).astype(kind)


def setup_inputs(seed: int = 0) -> dict:
    splits = jax.random.split(jax.random.key(seed), 8)
    return {
        "tokens": noise(splits[0], (TOKENS, MODEL_WIDTH), 1.0, 6.0, ((0, 32), (1, 4))),
        "norm_gain": jnp.clip(1.0 + 0.18 * jax.random.normal(splits[1], (MODEL_WIDTH,), jnp.float32), 0.1, 1.9),
        "segment_ids": jnp.searchsorted(jnp.cumsum(uneven_parts(splits[2], max(8, TOKENS // 256), TOKENS, TOKENS // 2 + 1, 1)), jnp.arange(TOKENS), side="right").astype(jnp.int32),
        "w_query": noise(splits[3], (MODEL_WIDTH, QUERY_HEADS * HEAD_SIZE), MODEL_WIDTH ** -0.5, 0.0625, ((0, 4), (1, 32))),
        "key_weight": noise(splits[4], (MODEL_WIDTH, KEY_VALUE_HEADS * HEAD_SIZE), MODEL_WIDTH ** -0.5, 0.0625, ((0, 4),)),
        "value_weight": noise(splits[5], (MODEL_WIDTH, KEY_VALUE_HEADS * HEAD_SIZE), MODEL_WIDTH ** -0.5, 0.0625, ((0, 4),)),
        "w_output": noise(splits[6], (QUERY_HEADS * HEAD_SIZE, MODEL_WIDTH), (QUERY_HEADS * HEAD_SIZE // 16) ** -0.5, 0.25, ((0, 32), (1, 4))),
    }


norm_eps = 1e-05
rope_base = 500000.0

def positions_of(segment_ids):
    length = segment_ids.shape[0]
    indices = jnp.arange(length, dtype=jnp.int32)
    changed = jnp.concatenate([jnp.ones((1,), jnp.bool_), segment_ids[1:] != segment_ids[:-1]])
    starts = lax.cummax(jnp.where(changed, indices, jnp.int32(0)), axis=0)
    return (indices - starts).astype(jnp.float32)

def rotate(values, places):
    half_dim = values.shape[-1] // 2
    freqs = jnp.exp(jnp.arange(half_dim, dtype=jnp.float32) * jnp.float32(-2.0 * math.log(rope_base) / values.shape[-1]))
    angles = places[:, None] * freqs[None, :]
    cosine = jnp.cos(angles)[:, None, :]
    sine = jnp.sin(angles)[:, None, :]
    first = values[..., :half_dim]
    second = values[..., half_dim:]
    return jnp.concatenate([first * cosine - second * sine, second * cosine + first * sine], axis=-1)

def reference(tokens, norm_gain, segment_ids, w_query, key_weight, value_weight, w_output):
    floats = tokens.astype(jnp.float32)
    scale_rows = lax.rsqrt(lax.optimization_barrier(jnp.mean(floats * floats, axis=-1, keepdims=True)) + norm_eps)
    normalized_input = (floats * scale_rows * norm_gain.astype(jnp.float32)[None, :]).astype(jnp.bfloat16)
    places = positions_of(segment_ids)
    row_total = tokens.shape[0]
    queries = jnp.dot(normalized_input, w_query, preferred_element_type=jnp.float32).reshape(row_total, QUERY_HEADS, HEAD_SIZE)
    key_states = jnp.dot(normalized_input, key_weight, preferred_element_type=jnp.float32).reshape(row_total, KEY_VALUE_HEADS, HEAD_SIZE)
    value_states = jnp.dot(normalized_input, value_weight, preferred_element_type=jnp.float32).reshape(row_total, KEY_VALUE_HEADS, HEAD_SIZE)
    queries16 = rotate(queries, places).astype(jnp.bfloat16)
    keys16 = rotate(key_states, places).astype(jnp.bfloat16)
    values16 = value_states.astype(jnp.bfloat16)
    indices = jnp.arange(row_total, dtype=jnp.int32)
    allowed = (segment_ids[:, None] == segment_ids[None, :]) & (indices[None, :] <= indices[:, None])
    score_scale = float(HEAD_SIZE) ** (-0.5)

    def one_head(head_number):
        query_group = head_number // (QUERY_HEADS // KEY_VALUE_HEADS)
        query_head = queries16[:, head_number]
        key_head = keys16[:, query_group]
        value_head = values16[:, query_group]
        scores = jnp.dot(query_head, key_head.T, preferred_element_type=jnp.float32) * score_scale
        masked = jnp.where(allowed, scores, -jnp.inf)
        highest = lax.optimization_barrier(jnp.max(masked, axis=-1, keepdims=True))
        probs = jnp.where(allowed, jnp.exp(masked - highest), jnp.float32(0.0))
        totals = lax.optimization_barrier(jnp.sum(probs, axis=-1, keepdims=True))
        mixed = jnp.dot(probs.astype(jnp.bfloat16), value_head, preferred_element_type=jnp.float32) / totals
        return mixed.astype(jnp.bfloat16)
    heads_out = lax.map(one_head, jnp.arange(QUERY_HEADS, dtype=jnp.int32))
    attended = jnp.transpose(heads_out, (1, 0, 2)).reshape(row_total, QUERY_HEADS * HEAD_SIZE)
    width_dev = QUERY_HEADS * HEAD_SIZE // N_TENSOR
    grouped = jnp.transpose(attended.reshape(row_total, N_TENSOR, width_dev), (1, 0, 2))
    weights_grouped = w_output.reshape(N_TENSOR, width_dev, MODEL_WIDTH)

    def add_group(summed, pair):
        part = jnp.dot(pair[0], pair[1], preferred_element_type=jnp.float32)
        rounded = lax.optimization_barrier(part.astype(jnp.bfloat16))
        return (summed + rounded.astype(jnp.float32), None)
    summed, unused = lax.scan(add_group, jnp.zeros((row_total, MODEL_WIDTH), jnp.float32), (grouped, weights_grouped))
    return summed.astype(jnp.bfloat16)
```

```python
import functools
import math

import jax
import jax.numpy as jnp
from jax import lax
from jax.experimental import pallas as pl
from jax.experimental.pallas import tpu as pltpu
from jax.sharding import Mesh, PartitionSpec as P

MODEL_WIDTH = 8192
QUERY_HEADS = 64
KEY_VALUE_HEADS = 8
HEAD_SIZE = 128
TOKENS = 4096
SEGMENTS = 16
GROUP_ROWS = 1024
TILE = 256

norm_eps = 1e-05
rope_base = 500000.0
MASKED = -1e30

f32 = jnp.float32
bf16 = jnp.bfloat16


def receive(value, axis, step):
    n = lax.axis_size(axis)
    return lax.ppermute(value, axis, [((i + step) % n, i) for i in range(n)])


def attention_kernel(scalars, q_ref, index_ref, start_ref, k0, k1, k2, v0, v1, v2, out_ref):
    dz = pl.program_id(0)
    y, z, xh = scalars[4], scalars[5], scalars[6]
    tile_low = scalars[dz]
    tile_high = y * 4 + lax.rem(z + dz, 4)
    q = jnp.concatenate([q_ref[:, :HEAD_SIZE], q_ref[:, HEAD_SIZE:]], axis=0)
    q_index = jnp.concatenate([index_ref[...], index_ref[...]], axis=0)
    q_start = jnp.concatenate([start_ref[...], start_ref[...]], axis=0)
    lane = lax.broadcasted_iota(jnp.int32, (1, TILE), 1) ^ (xh * 128)

    def step(k_ref, v_ref, tile, carry):
        top, total, acc = carry
        slot = lax.rem(lax.rem(tile, 4) - z + 4, 4) * TILE
        slot = pl.multiple_of(slot, TILE)
        k = k_ref[pl.ds(slot, TILE), :]
        v = v_ref[pl.ds(slot, TILE), :]
        s = lax.dot_general(q, k, (((1,), (1,)), ((), ())), preferred_element_type=f32)
        k_index = lane + tile * TILE
        allowed = (k_index <= q_index) & (k_index >= q_start)
        s = jnp.where(allowed, s, MASKED)
        new_top = jnp.maximum(top, jnp.max(s, axis=1, keepdims=True))
        p = jnp.exp2(s - new_top)
        decay = jnp.exp2(top - new_top)
        total = total * decay + jnp.sum(p, axis=1, keepdims=True)
        acc = acc * decay + jnp.dot(p.astype(bf16), v, preferred_element_type=f32)
        return new_top, total, acc

    carry = (
        jnp.full((2 * TILE, 1), MASKED, f32),
        jnp.zeros((2 * TILE, 1), f32),
        jnp.zeros((2 * TILE, HEAD_SIZE), f32),
    )
    for back, k_ref, v_ref in ((2, k2, v2), (1, k1, v1), (0, k0, v0)):
        first = (y - back) * 4
        low = jnp.maximum(tile_low, first)
        high = jnp.minimum(tile_high, first + 3)
        carry = lax.fori_loop(
            low, high + 1, functools.partial(step, k_ref, v_ref), carry
        )
    top, total, acc = carry
    result = (acc / total).astype(bf16)
    out_ref[:, :HEAD_SIZE] = result[:TILE]
    out_ref[:, HEAD_SIZE:] = result[TILE:]


def attention(scalars, q, index, start, keys, values):
    whole = pl.BlockSpec((GROUP_ROWS, HEAD_SIZE), lambda i: (0, 0))
    column = pl.BlockSpec((TILE, 1), lambda i: (i, 0))
    rows = pl.BlockSpec((TILE, 2 * HEAD_SIZE), lambda i: (i, 0))
    return pl.pallas_call(
        attention_kernel,
        grid=(4,),
        out_shape=jax.ShapeDtypeStruct((GROUP_ROWS, 2 * HEAD_SIZE), bf16),
        in_specs=[pl.BlockSpec(memory_space=pltpu.SMEM), rows, column, column] + [whole] * 6,
        out_specs=rows,
        compiler_params=pltpu.CompilerParams(vmem_limit_bytes=32 * 2**20),
        cost_estimate=pl.CostEstimate(flops=3 * 10**9, bytes_accessed=4 * 2**20, transcendentals=4 * 10**6),
    )(scalars, q, index, start, *keys, *values)


def rotate(values, cosine, sine):
    half = HEAD_SIZE // 2
    first, second = values[..., :half], values[..., half:]
    return jnp.concatenate([first * cosine - second * sine, second * cosine + first * sine], axis=-1)


def shards(tokens, norm_gain, segment_ids, w_query, key_weight, value_weight, w_output):
    xl, c, y, z, xh = (lax.axis_index(a) for a in ("xl", "c", "y", "z", "xh"))

    floats = tokens.astype(f32)
    scaled = (floats * norm_gain[None, :]).astype(bf16)
    x = {(0, 0): scaled}
    x[1, 0] = receive(scaled, "z", 1)
    x[3, 0] = receive(scaled, "z", -1)
    x[0, 1] = receive(scaled, "xh", 1)
    wq = {0: w_query}
    wq[1] = receive(w_query, "y", 1)
    wq[3] = receive(w_query, "y", -1)
    x[1, 1] = receive(x[0, 1], "z", 1)
    x[3, 1] = receive(x[0, 1], "z", -1)
    for dx in (0, 1):
        x[2, dx] = jnp.concatenate(
            [receive(x[1, dx][:64], "z", 1), receive(x[3, dx][64:], "z", -1)], axis=0
        )
    half = MODEL_WIDTH // 8
    wq[2] = jnp.concatenate([receive(wq[1][:half], "y", 1), receive(wq[3][half:], "y", -1)], axis=0)
    gathered = jnp.concatenate([x[dz, dx] for dz in range(4) for dx in range(2)], axis=0)

    squares = lax.psum(jnp.sum(floats * floats, axis=-1), ("xl", "c"))
    own_scale = lax.rsqrt(squares / MODEL_WIDTH + norm_eps)
    scale = lax.all_gather(own_scale, ("z", "xh"), axis=0, tiled=True).reshape(4, 2, 128)

    def relative(by_place):
        turned = lax.dynamic_slice_in_dim(jnp.concatenate([by_place, by_place], axis=0), z, 4, 0)
        return jnp.where(xh == 0, turned, turned[:, ::-1]).reshape(GROUP_ROWS)

    scale = relative(scale)[:, None]
    own_rows = lax.dynamic_slice_in_dim(segment_ids, y * GROUP_ROWS, GROUP_ROWS, 0)
    segments = relative(own_rows.reshape(4, 2, 128))
    index = relative((y * GROUP_ROWS + jnp.arange(GROUP_ROWS, dtype=jnp.int32)).reshape(4, 2, 128))
    ids = jnp.arange(SEGMENTS, dtype=jnp.int32)
    before = jnp.sum((segment_ids[None, :] < ids[:, None]).astype(jnp.int32), axis=1)
    start = jnp.sum(jnp.where(segments[:, None] == ids[None, :], before[None, :], 0), axis=1)
    places = (index - start).astype(f32)
    freqs = jnp.exp(jnp.arange(64, dtype=f32) * f32(-2.0 * math.log(rope_base) / HEAD_SIZE))
    angles = places[:, None] * freqs[None, :]
    cosine, sine = jnp.cos(angles) * scale, jnp.sin(angles) * scale

    def kv_weight(core):
        parts = []
        for other in (0, 1):
            which = (xl ^ other) * 4 + core * 2 + z // 2
            parts.append(lax.dynamic_slice_in_dim(key_weight, which * 128, 128, 1))
            parts.append(lax.dynamic_slice_in_dim(value_weight, which * 128, 128, 1))
        return jnp.concatenate(parts, axis=1)

    def summed_over_blk(weight_of, width):
        away = jnp.dot(gathered, weight_of(1 - c), preferred_element_type=f32).astype(bf16)
        got = receive(away, "c", 1)
        home = jnp.dot(gathered, weight_of(c), preferred_element_type=f32)
        both = home + got.astype(f32)
        far = receive(both[:, width:].astype(bf16), "xl", 1)
        return both[:, :width] + far.astype(f32)

    kv = summed_over_blk(kv_weight, 256)
    k_own = rotate(kv[:, :128], cosine, sine).astype(bf16)
    v_own = (kv[:, 128:] * scale).astype(bf16)
    k_1 = receive(k_own, "y", -1)
    v_1 = receive(v_own, "y", -1)
    v_up = receive(v_own, "y", 1)
    k_2 = receive(k_1, "y", -1)
    v_2 = receive(v_up, "y", 1)

    wq_all = jnp.stack([wq[i] for i in range(4)], axis=0)

    def query_weight(core):
        parts = []
        for other in (0, 1):
            which = lax.rem((xl ^ other) * 2 + core - y + 4, 4)
            parts.append(lax.dynamic_index_in_dim(wq_all, which, 0, keepdims=False))
        return jnp.concatenate(parts, axis=1)

    q = summed_over_blk(query_weight, 256)
    unit = f32(HEAD_SIZE ** (-0.5) * math.log2(math.e))
    q = rotate(
        q.reshape(GROUP_ROWS, 2, HEAD_SIZE), (cosine * unit)[:, None, :], (sine * unit)[:, None, :]
    ).reshape(GROUP_ROWS, 2 * HEAD_SIZE).astype(bf16)

    lows = jnp.min(start.reshape(4, TILE), axis=1) // TILE
    scalars = jnp.concatenate([lows, jnp.stack([y, z, xh, jnp.int32(0)])]).astype(jnp.int32)
    mixed = attention(
        scalars, q, index[:, None], start[:, None], (k_own, k_1, k_2), (v_own, v_1, v_2)
    )

    across = receive(mixed, "xl", 1)
    low, high = jnp.where(xl == 0, mixed, across), jnp.where(xl == 0, across, mixed)
    pair = jnp.concatenate([low, high], axis=1)
    other = receive(pair, "c", 1)
    even, odd = jnp.where(c == 0, pair, other), jnp.where(c == 0, other, pair)
    heads = jnp.concatenate([even[:, :256], odd[:, :256], even[:, 256:], odd[:, 256:]], axis=1)

    w_out_own, _ = lax.optimization_barrier((w_output, wq[2][:8, :128]))
    w_out = lax.all_gather(w_out_own, "y", axis=0, tiled=True)
    columns = w_out.shape[1] // 2

    def part(dz, side):
        return jnp.dot(
            heads[dz * TILE : (dz + 1) * TILE],
            w_out[:, side * columns : (side + 1) * columns],
            preferred_element_type=f32,
        )

    up = receive(part(2, 0).astype(bf16), "z", -1)
    down = receive(part(2, 1).astype(bf16), "z", 1)
    up_right = receive(part(1, 1).astype(bf16), "z", -1)
    down_left = receive(part(3, 0).astype(bf16), "z", 1)
    up_left = receive((part(1, 0) + up.astype(f32)).astype(bf16), "z", -1)
    down_right = receive((part(3, 1) + down.astype(f32)).astype(bf16), "z", 1)
    left = part(0, 0) + down_left.astype(f32) + up_left.astype(f32)
    right = part(0, 1) + up_right.astype(f32) + down_right.astype(f32)
    rows = jnp.concatenate([left, right], axis=1)
    last = receive(rows[128:].astype(bf16), "xh", 1)
    return (rows[:128] + last.astype(f32)).astype(bf16)


def solution(mesh):
    fine = Mesh(mesh.devices.reshape(2, 2, 4, 4, 2), ("xl", "c", "y", "z", "xh"))
    blk, tensor = ("xl", "c"), ("y", "z", "xh")
    placed = (
        P(tensor, blk),
        P(blk),
        P(),
        P(blk, tensor),
        P(blk, None),
        P(blk, None),
        P(tensor, blk),
    )
    return jax.shard_map(
        shards, mesh=fine, in_specs=placed, out_specs=P(tensor, blk), check_vma=False
    )
```

```python
import functools
import math

import jax
import jax.numpy as jnp
from jax import lax
from jax.experimental import pallas as pl
from jax.experimental.pallas import tpu as pltpu
from jax.sharding import Mesh, PartitionSpec as P

MODEL_WIDTH = 8192
QUERY_HEADS = 64
KEY_VALUE_HEADS = 8
HEAD_SIZE = 128
TOKENS = 4096
SEGMENTS = 16
GROUP_ROWS = 1024
TILE = 256
PART = 512

norm_eps = 1e-05
rope_base = 500000.0
MASKED = -1e30

f32 = jnp.float32
bf16 = jnp.bfloat16


def receive(value, axis, step):
    n = lax.axis_size(axis)
    return lax.ppermute(value, axis, [((i + step) % n, i) for i in range(n)])


def scale_rows(x_refs, gain_ref, scaled, squares=None):
    for i, ref in enumerate(x_refs):
        rows = pl.ds(i * 128, 128)
        floats = ref[...].astype(f32)
        scaled[rows, :] = (floats * gain_ref[...]).astype(bf16)
        if squares is not None:
            squares[:, rows] = lax.dot_general(
                jnp.ones((8, floats.shape[1]), bf16),
                (floats * floats).astype(bf16),
                (((1,), (1,)), ((), ())),
                preferred_element_type=f32,
            )


def kv_kernel(which, x0, x1, x2, x3, gain, key, value, out, squares, scaled):
    @pl.when(pl.program_id(0) == 0)
    def _():
        scale_rows((x0, x1, x2, x3), gain, scaled, squares)

    weight = jnp.concatenate([key[...], value[...]], axis=1)
    out[0] = jnp.dot(scaled[...], weight, preferred_element_type=f32).astype(bf16)


def project_kv(which, pieces, gain, key_weight, value_weight):
    depth = key_weight.shape[0]
    whole = pl.BlockSpec((128, depth), lambda j, w: (0, 0))
    column = pl.BlockSpec((depth, HEAD_SIZE), lambda j, w: (0, w[j]))
    return pl.pallas_call(
        kv_kernel,
        grid_spec=pltpu.PrefetchScalarGridSpec(
            num_scalar_prefetch=1,
            grid=(4,),
            in_specs=[whole] * 4 + [pl.BlockSpec((1, depth), lambda j, w: (0, 0)), column, column],
            out_specs=[
                pl.BlockSpec((1, PART, 2 * HEAD_SIZE), lambda j, w: (j, 0, 0)),
                pl.BlockSpec((8, PART), lambda j, w: (0, 0)),
            ],
            scratch_shapes=[pltpu.VMEM((PART, depth), bf16)],
        ),
        out_shape=[
            jax.ShapeDtypeStruct((4, PART, 2 * HEAD_SIZE), bf16),
            jax.ShapeDtypeStruct((8, PART), f32),
        ],
        compiler_params=pltpu.CompilerParams(vmem_limit_bytes=32 * 2**20),
        cost_estimate=pl.CostEstimate(flops=2 * PART * 2048 * 1024, bytes_accessed=8 * 2**20, transcendentals=0),
    )(which, *pieces, gain, key_weight, value_weight)


def query_kernel(place, x0, x1, x2, x3, x4, x5, x6, x7, gain, w0, w1, w2a, w2b, w3, out, scaled):
    step = pl.program_id(0)

    @pl.when(step == 0)
    def _():
        scale_rows((x0, x1, x2, x3, x4, x5, x6, x7), gain, scaled)

    for i, ref in ((0, w0), (1, w1), (3, w3)):

        @pl.when(step == i)
        def _():
            out[0] = jnp.dot(scaled[...], ref[...], preferred_element_type=f32).astype(bf16)

    @pl.when(step == 2)
    def _():
        half = w2a.shape[0]
        total = jnp.dot(scaled[:, :half], w2a[...], preferred_element_type=f32)
        total += jnp.dot(scaled[:, half:], w2b[...], preferred_element_type=f32)
        out[0] = total.astype(bf16)


def project_queries(place, pieces, gain, weights):
    depth, width = weights[0].shape
    return pl.pallas_call(
        query_kernel,
        grid_spec=pltpu.PrefetchScalarGridSpec(
            num_scalar_prefetch=1,
            grid=(4,),
            in_specs=[pl.BlockSpec(a.shape, lambda j, w: (0, 0)) for a in (*pieces, gain, *weights)],
            out_specs=pl.BlockSpec((1, GROUP_ROWS, width), lambda j, w: (w[j], 0, 0)),
            scratch_shapes=[pltpu.VMEM((GROUP_ROWS, depth), bf16)],
        ),
        out_shape=jax.ShapeDtypeStruct((4, GROUP_ROWS, width), bf16),
        compiler_params=pltpu.CompilerParams(vmem_limit_bytes=40 * 2**20),
        cost_estimate=pl.CostEstimate(
            flops=2 * GROUP_ROWS * 2048 * 1024, bytes_accessed=10 * 2**20, transcendentals=0
        ),
    )(place, *pieces, gain, *weights)


def turn(u, cosine, sine):
    return u * cosine + pltpu.roll(u, HEAD_SIZE // 2, 1) * sine


def finish_kernel(home, got, far, cosine, sine, columns, out):
    total = home[0].astype(f32) + got[0].astype(f32) + far[...].astype(f32)
    total = total * columns[:, 0:1]
    out[0] = turn(total[:, :HEAD_SIZE], cosine[...], sine[...]).astype(bf16)
    out[1] = total[:, HEAD_SIZE:].astype(bf16)


def finish_kv(out, got, far, cosine, sine, columns):
    wide = 2 * HEAD_SIZE
    rows = pl.BlockSpec((PART, HEAD_SIZE), lambda i: (0, 0))
    return pl.pallas_call(
        finish_kernel,
        grid=(1,),
        in_specs=[
            pl.BlockSpec((1, PART, wide), lambda i: (2, 0, 0)),
            pl.BlockSpec((1, PART, wide), lambda i: (0, 0, 0)),
            pl.BlockSpec((PART, wide), lambda i: (0, 0)),
            rows,
            rows,
            pl.BlockSpec((PART, 4), lambda i: (0, 0)),
        ],
        out_specs=pl.BlockSpec((2, PART, HEAD_SIZE), lambda i: (0, 0, 0)),
        out_shape=jax.ShapeDtypeStruct((2, PART, HEAD_SIZE), bf16),
        compiler_params=pltpu.CompilerParams(vmem_limit_bytes=16 * 2**20),
        cost_estimate=pl.CostEstimate(flops=PART * 2048, bytes_accessed=2 * 2**20, transcendentals=0),
    )(out, got, far, cosine, sine, columns)


def attention_kernel(
    scalars, home, got, far, cosine, sine, columns,
    own0, own1, up0, up1, k20, k21, v20, v21, out_ref, keys, values,
):
    dz = pl.program_id(0)
    y, z, xh = scalars[8], scalars[9], scalars[10]

    @pl.when(dz == 0)
    def _():
        for back, k_refs, v_refs in (
            (0, (own0.at[0], own1.at[0]), (own0.at[1], own1.at[1])),
            (1, (up0.at[0], up1.at[0]), (up0.at[1], up1.at[1])),
            (2, (k20, k21), (v20, v21)),
        ):
            for i in range(4):
                for dx in (0, 1):
                    at = ((2 - back) * 4 + lax.rem(z + i, 4)) * TILE + (xh ^ dx) * 128
                    at = pl.ds(pl.multiple_of(at, 128), 128)
                    keys[at, :] = k_refs[dx][i * 128 : (i + 1) * 128, :]
                    values[at, :] = v_refs[dx][i * 128 : (i + 1) * 128, :]

    def both(ref):
        return jnp.concatenate([ref[0], ref[1]], axis=0)

    cos, sin, cols = both(cosine), both(sine), both(columns)
    unit = f32(HEAD_SIZE ** (-0.5) * math.log2(math.e))
    raw = both(home[0]).astype(f32) + both(got[0]).astype(f32) + both(far).astype(f32)
    raw = raw * (cols[:, 0:1] * unit)
    q = jnp.concatenate(
        [turn(raw[:, :HEAD_SIZE], cos, sin), turn(raw[:, HEAD_SIZE:], cos, sin)], axis=0
    ).astype(bf16)
    shift = (y - 2) * GROUP_ROWS
    q_index = cols[:, 1:2].astype(jnp.int32) - shift
    q_start = cols[:, 2:3].astype(jnp.int32) - shift
    q_index = jnp.concatenate([q_index, q_index], axis=0)
    q_start = jnp.concatenate([q_start, q_start], axis=0)
    lane = lax.broadcasted_iota(jnp.int32, (1, TILE), 1)

    def step(masked, tile, carry):
        top, total, acc = carry
        at = pl.ds(pl.multiple_of(tile * TILE, TILE), TILE)
        s = lax.dot_general(q, keys[at, :], (((1,), (1,)), ((), ())), preferred_element_type=f32)
        if masked:
            k_index = lane + tile * TILE
            s = jnp.where((k_index <= q_index) & (k_index >= q_start), s, MASKED)
        new_top = jnp.maximum(top, jnp.max(s, axis=1, keepdims=True))
        p = jnp.exp2(s - new_top)
        decay = jnp.exp2(top - new_top)
        total = total * decay + jnp.sum(p, axis=1, keepdims=True)
        acc = acc * decay + jnp.dot(p.astype(bf16), values[at, :], preferred_element_type=f32)
        return new_top, total, acc

    carry = (
        jnp.full((2 * TILE, 1), MASKED, f32),
        jnp.zeros((2 * TILE, 1), f32),
        jnp.zeros((2 * TILE, HEAD_SIZE), f32),
    )
    last = 8 + lax.rem(z + dz, 4)
    first = jnp.maximum(scalars[dz] - shift // TILE, 0)
    clear = jnp.minimum(scalars[4 + dz] - shift // TILE, last)
    carry = lax.fori_loop(first, clear, functools.partial(step, True), carry)
    carry = lax.fori_loop(clear, last, functools.partial(step, False), carry)
    top, total, acc = step(True, last, carry)
    result = (acc / total).astype(bf16)
    for head in (0, 1):
        for dx in (0, 1):
            at = head * TILE + dx * 128
            out_ref[0, dx, :, head * HEAD_SIZE : (head + 1) * HEAD_SIZE] = result[at : at + 128]


def attention(scalars, out, got, far, cosine, sine, columns, own, up, k2, v2):
    wide = 2 * HEAD_SIZE
    out = out.reshape(4, 2, PART, wide)
    got = got.reshape(2, 2, PART, wide)
    far = far.reshape(2, PART, wide)
    two = pl.BlockSpec((2, PART, HEAD_SIZE), lambda i: (0, 0, 0))
    one = pl.BlockSpec((PART, HEAD_SIZE), lambda i: (0, 0))
    rows = pl.BlockSpec((2, 128, HEAD_SIZE), lambda i: (0, i, 0))
    return pl.pallas_call(
        attention_kernel,
        grid=(4,),
        in_specs=[
            pl.BlockSpec(memory_space=pltpu.SMEM),
            pl.BlockSpec((1, 2, 128, wide), lambda i: (2, 0, i, 0)),
            pl.BlockSpec((1, 2, 128, wide), lambda i: (0, 0, i, 0)),
            pl.BlockSpec((2, 128, wide), lambda i: (0, i, 0)),
            rows,
            rows,
            pl.BlockSpec((2, 128, 4), lambda i: (0, i, 0)),
        ]
        + [two] * 4
        + [one] * 4,
        out_specs=pl.BlockSpec((1, 2, 128, wide), lambda i: (i, 0, 0, 0)),
        out_shape=jax.ShapeDtypeStruct((4, 2, 128, wide), bf16),
        scratch_shapes=[pltpu.VMEM((3 * GROUP_ROWS, HEAD_SIZE), bf16)] * 2,
        compiler_params=pltpu.CompilerParams(vmem_limit_bytes=32 * 2**20),
        cost_estimate=pl.CostEstimate(flops=3 * 10**9, bytes_accessed=4 * 2**20, transcendentals=4 * 10**6),
    )(scalars, out, got, far, cosine, sine, columns, *own, *up, *k2, *v2)


def shards(tokens, norm_gain, segment_ids, w_query, key_weight, value_weight, w_output):
    xl, c, y, z, xh = (lax.axis_index(a) for a in ("xl", "c", "y", "z", "xh"))

    x = {(0, 0): tokens}
    x[1, 0] = receive(tokens, "z", 1)
    x[3, 0] = receive(tokens, "z", -1)
    x[0, 1] = receive(tokens, "xh", 1)
    w1 = receive(w_query, "y", 1)
    w3 = receive(w_query, "y", -1)
    x[2, 0] = jnp.concatenate(
        [receive(x[1, 0][:64], "z", 1), receive(x[3, 0][64:], "z", -1)], axis=0
    )
    near, x[2, 0] = lax.optimization_barrier((x[0, 1], x[2, 0]))
    x[1, 1] = receive(near, "z", 1)
    x[3, 1] = receive(near, "z", -1)
    x[2, 1] = receive(x[2, 0], "xh", 1)
    half = w_query.shape[0] // 2
    w2a = receive(w1[:half], "y", 1)
    w2b = receive(w3[half:], "y", -1)
    w_out_own, w2a, w2b = lax.optimization_barrier((w_output, w2a, w2b))
    w_out = lax.all_gather(w_out_own, "y", axis=0, tiled=True)

    def relative(by_place):
        turned = lax.dynamic_slice_in_dim(jnp.concatenate([by_place, by_place], axis=0), z, 4, 0)
        swapped = jnp.where(xh == 0, turned, turned[:, ::-1])
        return jnp.transpose(swapped, (1, 0, 2)).reshape(2, PART)

    own_rows = lax.dynamic_slice_in_dim(segment_ids, y * GROUP_ROWS, GROUP_ROWS, 0)
    segments = relative(own_rows.reshape(4, 2, 128))
    index = relative((y * GROUP_ROWS + jnp.arange(GROUP_ROWS, dtype=jnp.int32)).reshape(4, 2, 128))
    ids = jnp.arange(SEGMENTS, dtype=jnp.int32)
    before = jnp.sum((segment_ids[None, :] < ids[:, None]).astype(jnp.int32), axis=1)
    start = jnp.sum(jnp.where(segments[None] == ids[:, None, None], before[:, None, None], 0), axis=0)
    places = (index - start).astype(f32)
    freqs = jnp.exp(jnp.arange(64, dtype=f32) * f32(-2.0 * math.log(rope_base) / HEAD_SIZE))
    angles = places[:, :, None] * freqs
    cosine, sine = jnp.cos(angles), jnp.sin(angles)
    cosine = jnp.concatenate([cosine, cosine], axis=2)
    sine = jnp.concatenate([-sine, sine], axis=2)
    by_tile = start.reshape(2, 4, 128)
    lows = jnp.min(by_tile, axis=(0, 2)) // TILE
    clears = (jnp.max(by_tile, axis=(0, 2)) + TILE - 1) // TILE
    zero = jnp.int32(0)
    scalars = jnp.concatenate([lows, clears, jnp.stack([y, z, xh, zero])]).astype(jnp.int32)

    def gather_blk_sum(out):
        got = receive(out[:2], "c", 1)
        far = receive((out[3].astype(f32) + got[1].astype(f32)).astype(bf16), "xl", 1)
        return got, far

    gain = norm_gain[None, :]
    targets = [(xl * 2 + (1 - c)), ((1 - xl) * 2 + (1 - c)), (xl * 2 + c), ((1 - xl) * 2 + c)]
    which = jnp.stack([b * 2 + z // 2 for b in targets]).astype(jnp.int32)
    own, up, k2, v2, columns = [], [], [], [], []
    for dx in (0, 1):
        out, squares = project_kv(which, [x[dz, dx] for dz in range(4)], gain, key_weight, value_weight)
        got, far = gather_blk_sum(out)
        squares = squares + receive(squares, "c", 1)
        squares = squares + receive(squares, "xl", 1)
        scale = lax.rsqrt(squares[0] / MODEL_WIDTH + norm_eps)
        columns.append(
            jnp.stack([scale, index[dx].astype(f32), start[dx].astype(f32), jnp.zeros_like(scale)], axis=1)
        )
        kv = finish_kv(out, got, far, cosine[dx], sine[dx], columns[dx])
        one_up = receive(kv, "y", -1)
        v_down = receive(kv[1], "y", 1)
        own.append(kv)
        up.append(one_up)
        k2.append(receive(one_up[0], "y", -1))
        v2.append(receive(v_down, "y", 1))

    place = []
    for i in range(4):
        b = lax.rem(y + i, 4)
        place.append(jnp.where(b % 2 == c, 2, 0) + jnp.where(b // 2 == xl, 0, 1))
    place = jnp.stack(place).astype(jnp.int32)
    out = project_queries(
        place, [x[dz, dx] for dx in (0, 1) for dz in range(4)], gain, (w_query, w1, w2a, w2b, w3)
    )
    got, far = gather_blk_sum(out)
    mixed = attention(
        scalars, out, got, far, cosine, sine, jnp.stack(columns), own, up, k2, v2
    ).reshape(GROUP_ROWS, 2 * HEAD_SIZE)

    across = receive(mixed, "xl", 1)
    low, high = jnp.where(xl == 0, mixed, across), jnp.where(xl == 0, across, mixed)
    pair = jnp.concatenate([low, high], axis=1)
    other = receive(pair, "c", 1)
    even, odd = jnp.where(c == 0, pair, other), jnp.where(c == 0, other, pair)
    heads = jnp.concatenate([even[:, :256], odd[:, :256], even[:, 256:], odd[:, 256:]], axis=1)

    columns = w_out.shape[1] // 2

    def part(dz, side):
        return jnp.dot(
            heads[dz * TILE : (dz + 1) * TILE],
            w_out[:, side * columns : (side + 1) * columns],
            preferred_element_type=f32,
        )

    up = receive(part(2, 0).astype(bf16), "z", -1)
    down = receive(part(2, 1).astype(bf16), "z", 1)
    up_right = receive(part(1, 1).astype(bf16), "z", -1)
    down_left = receive(part(3, 0).astype(bf16), "z", 1)
    up_left = receive((part(1, 0) + up.astype(f32)).astype(bf16), "z", -1)
    down_right = receive((part(3, 1) + down.astype(f32)).astype(bf16), "z", 1)
    left = part(0, 0) + down_left.astype(f32) + up_left.astype(f32)
    right = part(0, 1) + up_right.astype(f32) + down_right.astype(f32)
    rows = jnp.concatenate([left, right], axis=1)
    last = receive(rows[128:].astype(bf16), "xh", 1)
    return (rows[:128] + last.astype(f32)).astype(bf16)


def solution(mesh):
    fine = Mesh(mesh.devices.reshape(2, 2, 4, 4, 2), ("xl", "c", "y", "z", "xh"))
    blk, tensor = ("xl", "c"), ("y", "z", "xh")
    placed = (
        P(tensor, blk),
        P(blk),
        P(),
        P(blk, tensor),
        P(blk, None),
        P(blk, None),
        P(tensor, blk),
    )
    return jax.shard_map(
        shards, mesh=fine, in_specs=placed, out_specs=P(tensor, blk), check_vma=False
    )
```

```python
import functools
import math

import jax
import jax.numpy as jnp
from jax import lax
from jax.experimental import pallas as pl
from jax.experimental.pallas import tpu as pltpu
from jax.sharding import Mesh, PartitionSpec as P

MODEL_WIDTH = 8192
QUERY_HEADS = 64
KEY_VALUE_HEADS = 8
HEAD_SIZE = 128
TOKENS = 4096
SEGMENTS = 16
GROUP_ROWS = 1024
TILE = 256
PART = 512
WIDE = 2 * HEAD_SIZE

norm_eps = 1e-05
rope_base = 500000.0
MASKED = -1e30
VMEM = 60 * 2**20

f32 = jnp.float32
bf16 = jnp.bfloat16


def receive(value, axis, step):
    n = lax.axis_size(axis)
    return lax.ppermute(value, axis, [((i + step) % n, i) for i in range(n)])


def turn(u, cosine, sine):
    return u * cosine + pltpu.roll(u, HEAD_SIZE // 2, 1) * sine


def finish_kernel(core, home, far, cosine, sine, scale, out):
    total = (home[...].astype(f32) + far[...].astype(f32)) * scale[...]
    out[0] = turn(total[:, :HEAD_SIZE], cosine[0], sine[0]).astype(bf16)
    out[1] = total[:, HEAD_SIZE:].astype(bf16)


def finish_kv(core, home, far, cosine, sine, scale):
    rows = pl.BlockSpec((PART, WIDE), lambda i, core: (0, 0))
    angle = pl.BlockSpec((1, PART, HEAD_SIZE), lambda i, core: (core[0], 0, 0))
    return pl.pallas_call(
        finish_kernel,
        grid_spec=pltpu.PrefetchScalarGridSpec(
            num_scalar_prefetch=1,
            grid=(1,),
            in_specs=[rows, rows, angle, angle, pl.BlockSpec((PART, 1), lambda i, core: (core[0], 0))],
            out_specs=pl.BlockSpec((2, PART, HEAD_SIZE), lambda i, core: (0, 0, 0)),
        ),
        out_shape=jax.ShapeDtypeStruct((2, PART, HEAD_SIZE), bf16),
        compiler_params=pltpu.CompilerParams(vmem_limit_bytes=VMEM),
        cost_estimate=pl.CostEstimate(flops=PART * 2048, bytes_accessed=2 * 2**20, transcendentals=0),
    )(core, home, far, cosine, sine, scale)


def attention_kernel(
    tiles, scalars, home0, home1, far0, far1, cosine, sine, scale0, scale1, bounds,
    m0, m1, m2, m3, t0, t1, t2, t3, out_ref, keys, values,
):
    place = pl.program_id(0)
    dy = jnp.where(place == 0, tiles[0], tiles[1])
    y, z, xh, c = scalars[8], scalars[9], scalars[10], scalars[11]

    @pl.when(place == 0)
    def _():
        for halves, dx in (((m0, m1, m2, m3), c), ((t0, t1, t2, t3), 1 - c)):
            for dz, ref in enumerate(halves):
                for i in range(4):
                    at = (lax.rem(y + i, 4) * 4 + lax.rem(z + dz, 4)) * TILE + (xh ^ dx) * 128
                    at = pl.ds(pl.multiple_of(at, 128), 128)
                    keys[at, :] = ref[0, i * 128 : (i + 1) * 128, :]
                    values[at, :] = ref[1, i * 128 : (i + 1) * 128, :]

    unit = f32(HEAD_SIZE ** (-0.5) * math.log2(math.e))
    turned = []
    for dx, (home, far, scale) in enumerate(((home0, far0, scale0), (home1, far1, scale1))):
        raw = (home[...].astype(f32) + far[...].astype(f32)) * (scale[...] * unit)
        for head in (0, 1):
            u = raw[:, head * HEAD_SIZE : (head + 1) * HEAD_SIZE]
            turned.append(turn(u, cosine[dx], sine[dx]).astype(bf16))
    q = jnp.concatenate([turned[0], turned[2], turned[1], turned[3]], axis=0)
    q_index = bounds[0, 0:1, :]
    q_start = bounds[0, 1:2, :]

    def step(masked, width, tile, carry):
        top, total, acc = carry
        first_key = tile * width
        at = pl.ds(pl.multiple_of(first_key, TILE), width)
        s = lax.dot_general(keys[at, :], q, (((1,), (1,)), ((), ())), preferred_element_type=f32)
        if masked:
            k_index = lax.broadcasted_iota(jnp.int32, (width, 1), 0) + first_key
            s = jnp.where((k_index <= q_index) & (k_index >= q_start), s, MASKED)
        new_top = jnp.maximum(top, jnp.max(s, axis=0, keepdims=True))
        p = jnp.exp2(s - new_top)
        decay = jnp.exp2(top - new_top)
        total = total * decay + jnp.sum(p, axis=0, keepdims=True)
        added = lax.dot_general(
            values[at, :], p.astype(bf16), (((0,), (0,)), ((), ())), preferred_element_type=f32
        )
        return new_top, total, acc * decay + added

    carry = (
        jnp.full((1, 2 * TILE), MASKED, f32),
        jnp.zeros((1, 2 * TILE), f32),
        jnp.zeros((HEAD_SIZE, 2 * TILE), f32),
    )
    last = lax.rem(y + dy, 4) * 4 + z
    first = scalars[dy]
    clear = jnp.minimum(scalars[4 + dy], last)
    big = 4
    big_first = (clear + big - 1) // big
    big_last = jnp.maximum(last // big, big_first)
    middle = jnp.minimum(big_first * big, last)
    one = functools.partial(step, False, TILE)
    carry = lax.fori_loop(first, clear, functools.partial(step, True, TILE), carry)
    carry = lax.fori_loop(clear, middle, one, carry)
    carry = lax.fori_loop(big_first, big_last, functools.partial(step, False, big * TILE), carry)
    carry = lax.fori_loop(jnp.maximum(big_last * big, middle), last, one, carry)
    top, total, acc = step(True, TILE, last, carry)
    result = (acc / total).T.astype(bf16)
    for head in (0, 1):
        for dx in (0, 1):
            at = head * TILE + dx * 128
            out_ref[0, dx, :, head * HEAD_SIZE : (head + 1) * HEAD_SIZE] = result[at : at + 128]


def attention(tiles, scalars, home, far, cosine, sine, scale, bounds, mine, theirs):
    def tile(i):
        return jnp.where(i == 0, tiles[0], tiles[1])

    half = pl.BlockSpec((2, PART, HEAD_SIZE), lambda i: (0, 0, 0))
    rows = [pl.BlockSpec((128, WIDE), lambda i, dx=dx: (4 * dx + tile(i), 0)) for dx in (0, 1)]
    angle = pl.BlockSpec((2, 128, HEAD_SIZE), lambda i: (0, tile(i), 0))
    column = [pl.BlockSpec((128, 1), lambda i, dx=dx: (4 * dx + tile(i), 0)) for dx in (0, 1)]
    return pl.pallas_call(
        functools.partial(attention_kernel, tiles),
        grid=(2,),
        in_specs=[pl.BlockSpec(memory_space=pltpu.SMEM)]
        + rows * 2
        + [angle] * 2
        + column
        + [pl.BlockSpec((1, 2, 2 * TILE), lambda i: (tile(i), 0, 0))]
        + [half] * 8,
        out_specs=pl.BlockSpec((1, 2, 128, WIDE), lambda i: (i, 0, 0, 0)),
        out_shape=jax.ShapeDtypeStruct((2, 2, 128, WIDE), bf16),
        scratch_shapes=[pltpu.VMEM((TOKENS, HEAD_SIZE), bf16)] * 2,
        compiler_params=pltpu.CompilerParams(vmem_limit_bytes=VMEM),
        cost_estimate=pl.CostEstimate(
            flops=3 * 10**9, bytes_accessed=4 * 2**20, transcendentals=4 * 10**6
        ),
    )(scalars, home, home, far, far, cosine, sine, scale, scale, bounds, *mine, *theirs)


def shards(tokens, norm_gain, segment_ids, w_query, key_weight, value_weight, w_output):
    xl, c, y, z, xh = (lax.axis_index(a) for a in ("xl", "c", "y", "z", "xh"))
    barrier = lax.optimization_barrier

    x = {(0, 0): tokens}
    x[1, 0] = receive(tokens, "y", 1)
    x[3, 0] = receive(tokens, "y", -1)
    x[0, 1] = receive(tokens, "xh", 1)
    x[2, 0] = receive(tokens, "y", 2)
    key_weight, value_weight, segment_ids, x[0, 1] = barrier(
        (key_weight, value_weight, segment_ids, x[0, 1])
    )
    x[1, 1] = receive(x[0, 1], "y", 1)
    x[3, 1] = receive(x[0, 1], "y", -1)
    x[2, 1] = receive(x[2, 0], "xh", 1)

    weights = lax.all_gather(w_query, "z", axis=0, tiled=True)
    w_output, weights = barrier((w_output, weights))
    weights = weights.reshape(4, w_query.shape[0], w_query.shape[1])
    w_out = lax.all_gather(w_output, "z", axis=0, tiled=True)

    def relative(by_place):
        turned = lax.dynamic_slice_in_dim(jnp.concatenate([by_place, by_place], axis=0), y, 4, 0)
        swapped = jnp.where(xh == 0, turned, turned[:, ::-1])
        return jnp.transpose(swapped, (1, 0, 2)).reshape(2, PART)

    def own_rows(values):
        return relative(lax.dynamic_index_in_dim(values.reshape(4, 4, 2, 128), z, 1, keepdims=False))

    segments = own_rows(segment_ids)
    index = own_rows(jnp.arange(TOKENS, dtype=jnp.int32))
    ids = jnp.arange(SEGMENTS, dtype=jnp.int32)
    before = jnp.sum((segment_ids[None, :] < ids[:, None]).astype(jnp.int32), axis=1)
    start = jnp.sum(jnp.where(segments[None] == ids[:, None, None], before[:, None, None], 0), axis=0)
    places = (index - start).astype(f32)
    freqs = jnp.exp(jnp.arange(64, dtype=f32) * f32(-2.0 * math.log(rope_base) / HEAD_SIZE))
    angles = places[:, :, None] * freqs
    cosine, sine = jnp.cos(angles), jnp.sin(angles)
    cosine = jnp.concatenate([cosine, cosine], axis=2)
    sine = jnp.concatenate([-sine, sine], axis=2)
    by_tile = start.reshape(2, 4, 128)
    lows = jnp.min(by_tile, axis=(0, 2)) // TILE
    clears = (jnp.max(by_tile, axis=(0, 2)) + TILE - 1) // TILE
    scalars = jnp.concatenate([lows, clears, jnp.stack([y, z, xh, c])]).astype(jnp.int32)

    def per_tile(values):
        rows = jnp.transpose(values.reshape(2, 4, 128), (1, 0, 2)).reshape(4, TILE)
        return jnp.concatenate([rows, rows], axis=1)

    bounds = jnp.stack([per_tile(index), per_tile(start)], axis=1)

    def kv_weight(across):
        which = y * 2 + (xl ^ across)
        parts = [lax.dynamic_slice_in_dim(w, which * 128, 128, 1) for w in (key_weight, value_weight)]
        return jnp.concatenate(parts, axis=1)

    kv_weights = barrier([kv_weight(0), kv_weight(1)])
    gain = norm_gain[None, :]
    pieces = [x[dy, dx].astype(f32) for dx in (0, 1) for dy in range(4)]
    rows = jnp.concatenate([(piece * gain).astype(bf16) for piece in pieces], axis=0)
    squares = jnp.stack([jnp.sum(piece * piece, axis=1) for piece in pieces])

    def half(rows, core):
        return lax.dynamic_slice_in_dim(rows, core * PART, PART, 0)

    def product(rows, weight):
        return jnp.dot(rows, weight, preferred_element_type=f32)

    away = half(rows, 1 - c)
    got_across = receive(product(away, kv_weights[1]).astype(bf16), "c", 1)
    got = receive(product(away, kv_weights[0]).astype(bf16), "c", 1)
    across = (product(half(rows, c), kv_weights[1]) + got_across.astype(f32)).astype(bf16)
    rows, across, squares = barrier((rows, across, squares))
    kv_far = receive(across, "xl", 1)
    kv_home = (product(half(rows, c), kv_weights[0]) + got.astype(f32)).astype(bf16)
    squares = squares + receive(squares, "c", 1)
    squares = squares + receive(squares, "xl", 1)
    scale = lax.rsqrt(squares.reshape(GROUP_ROWS, 1) / MODEL_WIDTH + norm_eps)
    kv = finish_kv(c.astype(jnp.int32)[None], kv_home, kv_far, cosine, sine, scale)
    mine = [kv] + [receive(kv, "z", step) for step in (1, 2, 3)]
    theirs = [receive(part, "c", 1) for part in mine]

    rows, kv_home = barrier((rows, kv_home))

    def query_weight(core, across):
        return lax.dynamic_index_in_dim(weights, (xl ^ across) * 2 + core, 0, keepdims=False)

    got_across = receive(product(rows, query_weight(1 - c, 1)).astype(bf16), "c", 1)
    got = receive(product(rows, query_weight(1 - c, 0)).astype(bf16), "c", 1)
    across = (product(rows, query_weight(c, 1)) + got_across.astype(f32)).astype(bf16)
    rows, across = barrier((rows, across))
    q_far = receive(across, "xl", 1)
    q_home = (product(rows, query_weight(c, 0)) + got.astype(f32)).astype(bf16)

    def all_heads(mixed, before):
        across = receive(mixed, "xl", 1)
        if before:
            across, *before = barrier((across, *before))
        low, high = jnp.where(xl == 0, mixed, across), jnp.where(xl == 0, across, mixed)
        pair = jnp.concatenate([low, high], axis=1)
        other = receive(pair, "c", 1)
        even, odd = jnp.where(c == 0, pair, other), jnp.where(c == 0, other, pair)
        heads = jnp.concatenate([even[:, :WIDE], odd[:, :WIDE], even[:, WIDE:], odd[:, WIDE:]], axis=1)
        return heads, before

    columns = w_out.shape[1] // 2
    y_first, xh_first = {}, {}
    mixed = [
        attention(tiles, scalars, q_home, q_far, cosine, sine, scale, bounds, mine, theirs)
        for tiles in ((2, 3), (1, 0))
    ]
    sent, seconds = [mixed[1]], []
    for step, tiles in enumerate(((2, 3), (1, 0))):
        heads, sent = all_heads(mixed[step].reshape(PART, WIDE), sent)
        if step == 0:
            mixed[1] = sent[0]
        else:
            y_first[2], y_first[3], seconds[0] = sent
        for i, dy in enumerate(tiles):
            y_first[dy] = jnp.dot(
                heads[i * TILE : (i + 1) * TILE], w_out[:, :columns], preferred_element_type=f32
            ).astype(bf16)
        seconds.append(jnp.dot(heads, w_out[:, columns:], preferred_element_type=f32).astype(bf16))
        sent = [y_first[tiles[0]], y_first[tiles[1]], seconds[-1]]
    for step, tiles in enumerate(((2, 3), (1, 0))):
        second = seconds[step].reshape(2, 2, 128, columns)
        got = receive(second[:, 1], "xh", 1)
        if step == 1:
            got, xh_first[2], xh_first[3] = barrier((got, xh_first[2], xh_first[3]))
        for i, dy in enumerate(tiles):
            xh_first[dy] = (second[i, 0].astype(f32) + got[i].astype(f32)).astype(bf16)

    def sum_over_y(parts):
        total = parts[0].astype(f32)
        for dy in (2, 3, 1):
            total = total + receive(parts[dy], "y", -dy).astype(f32)
        return total

    first = sum_over_y(y_first)
    second = sum_over_y(xh_first)
    first = first[:128] + receive(first[128:].astype(bf16), "xh", 1).astype(f32)
    return jnp.concatenate([first, second], axis=1).astype(bf16)


def solution(mesh):
    fine = Mesh(mesh.devices.reshape(2, 2, 4, 4, 2), ("xl", "c", "y", "z", "xh"))
    blk, tensor = ("xl", "c"), ("y", "z", "xh")
    placed = (
        P(tensor, blk),
        P(blk),
        P(),
        P(blk, tensor),
        P(blk, None),
        P(blk, None),
        P(tensor, blk),
    )
    return jax.shard_map(
        shards, mesh=fine, in_specs=placed, out_specs=P(tensor, blk), check_vma=False
    )
```

```python
import functools
import math

import jax
import jax.numpy as jnp
from jax import lax
from jax.experimental import pallas as pl
from jax.experimental.pallas import tpu as pltpu
from jax.sharding import Mesh, PartitionSpec as P

MODEL_WIDTH = 8192
QUERY_HEADS = 64
KEY_VALUE_HEADS = 8
HEAD_SIZE = 128
TOKENS = 4096
SEGMENTS = 16
GROUP_ROWS = 1024
TILE = 256
PART = 512
WIDE = 2 * HEAD_SIZE

norm_eps = 1e-05
rope_base = 500000.0
MASKED = -1e30
VMEM = 60 * 2**20
LIGHT = pl.CostEstimate(flops=1, bytes_accessed=1, transcendentals=0)

f32 = jnp.float32
bf16 = jnp.bfloat16


def receive(value, axis, step):
    n = lax.axis_size(axis)
    return lax.ppermute(value, axis, [((i + step) % n, i) for i in range(n)])


def turn(u, cosine, sine):
    return u * cosine + pltpu.roll(u, HEAD_SIZE // 2, 1) * sine


def pick(tiles, i):
    chosen = jnp.int32(tiles[0])
    for at, tile in enumerate(tiles[1:], 1):
        chosen = jnp.where(i == at, jnp.int32(tile), chosen)
    return chosen


def attention_kernel(
    tiles, scalars, home0, home1, far0, far1, cosine, sine, scale0, scale1, bounds,
    m0, m1, m2, m3, t0, t1, t2, t3, out_ref, keys, values,
):
    place = pl.program_id(0)
    dy = pick(tiles, place)
    y, z, xh, c = scalars[8], scalars[9], scalars[10], scalars[11]

    @pl.when(place == 0)
    def _():
        for halves, dx in (((m0, m1, m2, m3), c), ((t0, t1, t2, t3), 1 - c)):
            for dz, ref in enumerate(halves):
                for i in range(4):
                    at = (lax.rem(y + i, 4) * 4 + lax.rem(z + dz, 4)) * TILE + (xh ^ dx) * 128
                    at = pl.ds(pl.multiple_of(at, 128), 128)
                    keys[at, :] = ref[0, i * 128 : (i + 1) * 128, :]
                    values[at, :] = ref[1, i * 128 : (i + 1) * 128, :]

    unit = f32(HEAD_SIZE ** (-0.5) * math.log2(math.e))
    turned = []
    for dx, (home, far, scale) in enumerate(((home0, far0, scale0), (home1, far1, scale1))):
        raw = (home[...].astype(f32) + far[...].astype(f32)) * (scale[...] * unit)
        for head in (0, 1):
            u = raw[:, head * HEAD_SIZE : (head + 1) * HEAD_SIZE]
            turned.append(turn(u, cosine[dx], sine[dx]).astype(bf16))
    q = jnp.concatenate([turned[0], turned[2], turned[1], turned[3]], axis=0)
    q_index = bounds[0, 0:1, :]
    q_start = bounds[0, 1:2, :]

    def step(masked, width, tile, carry):
        top, total, acc = carry
        first_key = tile * width
        at = pl.ds(pl.multiple_of(first_key, TILE), width)
        s = lax.dot_general(keys[at, :], q, (((1,), (1,)), ((), ())), preferred_element_type=f32)
        if masked:
            k_index = lax.broadcasted_iota(jnp.int32, (width, 1), 0) + first_key
            s = jnp.where((k_index <= q_index) & (k_index >= q_start), s, MASKED)
        new_top = jnp.maximum(top, jnp.max(s, axis=0, keepdims=True))
        p = jnp.exp2(s - new_top)
        decay = jnp.exp2(top - new_top)
        total = total * decay + jnp.sum(p, axis=0, keepdims=True)
        added = lax.dot_general(
            values[at, :], p.astype(bf16), (((0,), (0,)), ((), ())), preferred_element_type=f32
        )
        return new_top, total, acc * decay + added

    carry = (
        jnp.full((1, 2 * TILE), MASKED, f32),
        jnp.zeros((1, 2 * TILE), f32),
        jnp.zeros((HEAD_SIZE, 2 * TILE), f32),
    )
    last = lax.rem(y + dy, 4) * 4 + z
    first = scalars[dy]
    clear = jnp.minimum(scalars[4 + dy], last)
    big = 4
    big_first = (clear + big - 1) // big
    big_last = jnp.maximum(last // big, big_first)
    middle = jnp.minimum(big_first * big, last)
    one = functools.partial(step, False, TILE)
    carry = lax.fori_loop(first, clear, functools.partial(step, True, TILE), carry)
    carry = lax.fori_loop(clear, middle, one, carry)
    carry = lax.fori_loop(big_first, big_last, functools.partial(step, False, big * TILE), carry)
    carry = lax.fori_loop(jnp.maximum(big_last * big, middle), last, one, carry)
    top, total, acc = step(True, TILE, last, carry)
    result = (acc / total).T.astype(bf16)
    for head in (0, 1):
        for dx in (0, 1):
            at = head * TILE + dx * 128
            out_ref[0, dx, :, head * HEAD_SIZE : (head + 1) * HEAD_SIZE] = result[at : at + 128]


def attention(tiles, scalars, home, far, cosine, sine, scale, bounds, mine, theirs):
    def tile(i):
        return pick(tiles, i)

    half = pl.BlockSpec((2, PART, HEAD_SIZE), lambda i: (0, 0, 0))
    rows = [pl.BlockSpec((128, WIDE), lambda i, dx=dx: (4 * dx + tile(i), 0)) for dx in (0, 1)]
    angle = pl.BlockSpec((2, 128, HEAD_SIZE), lambda i: (0, tile(i), 0))
    column = [pl.BlockSpec((128, 1), lambda i, dx=dx: (4 * dx + tile(i), 0)) for dx in (0, 1)]
    return pl.pallas_call(
        functools.partial(attention_kernel, tiles),
        grid=(len(tiles),),
        in_specs=[pl.BlockSpec(memory_space=pltpu.SMEM)]
        + rows * 2
        + [angle] * 2
        + column
        + [pl.BlockSpec((1, 2, 2 * TILE), lambda i: (tile(i), 0, 0))]
        + [half] * 8,
        out_specs=pl.BlockSpec((1, 2, 128, WIDE), lambda i: (i, 0, 0, 0)),
        out_shape=jax.ShapeDtypeStruct((len(tiles), 2, 128, WIDE), bf16),
        scratch_shapes=[pltpu.VMEM((TOKENS, HEAD_SIZE), bf16)] * 2,
        compiler_params=pltpu.CompilerParams(vmem_limit_bytes=VMEM),
        cost_estimate=pl.CostEstimate(
            flops=len(tiles) * 10**9, bytes_accessed=2**22, transcendentals=len(tiles) * 10**6
        ),
    )(scalars, home, home, far, far, cosine, sine, scale, scale, bounds, *mine, *theirs)


def shards(tokens, norm_gain, segment_ids, w_query, key_weight, value_weight, w_output):
    xl, c, y, z, xh = (lax.axis_index(a) for a in ("xl", "c", "y", "z", "xh"))
    barrier = lax.optimization_barrier

    x = {(0, 0): tokens}
    x[1, 0] = receive(tokens, "y", 1)
    x[3, 0] = receive(tokens, "y", -1)
    x[0, 1] = receive(tokens, "xh", 1)
    x[2, 0] = receive(tokens, "y", 2)
    key_weight, value_weight, segment_ids, w_output, x[0, 1] = barrier(
        (key_weight, value_weight, segment_ids, w_output, x[0, 1])
    )
    x[1, 1] = receive(x[0, 1], "y", 1)
    x[3, 1] = receive(x[0, 1], "y", -1)
    x[2, 1] = receive(x[2, 0], "xh", 1)

    weights = lax.all_gather(w_query, "z", axis=0, tiled=True)
    w_out = lax.all_gather(w_output, "z", axis=0, tiled=True)
    columns = w_output.shape[1] // 2
    def relative(by_place):
        turned = lax.dynamic_slice_in_dim(jnp.concatenate([by_place, by_place], axis=0), y, 4, 0)
        swapped = jnp.where(xh == 0, turned, turned[:, ::-1])
        return jnp.transpose(swapped, (1, 0, 2)).reshape(2, PART)

    def own_rows(values):
        return relative(lax.dynamic_index_in_dim(values.reshape(4, 4, 2, 128), z, 1, keepdims=False))

    segments = own_rows(segment_ids)
    index = own_rows(jnp.arange(TOKENS, dtype=jnp.int32))
    ids = jnp.arange(SEGMENTS, dtype=jnp.int32)
    before = jnp.sum((segment_ids[None, :] < ids[:, None]).astype(jnp.int32), axis=1)
    start = jnp.sum(jnp.where(segments[None] == ids[:, None, None], before[:, None, None], 0), axis=0)
    places = (index - start).astype(f32)
    freqs = jnp.exp(jnp.arange(64, dtype=f32) * f32(-2.0 * math.log(rope_base) / HEAD_SIZE))
    angles = places[:, :, None] * freqs
    cosine, sine = jnp.cos(angles), jnp.sin(angles)
    cosine = jnp.concatenate([cosine, cosine], axis=2)
    sine = jnp.concatenate([-sine, sine], axis=2)
    by_tile = start.reshape(2, 4, 128)
    lows = jnp.min(by_tile, axis=(0, 2)) // TILE
    clears = (jnp.max(by_tile, axis=(0, 2)) + TILE - 1) // TILE
    scalars = jnp.concatenate([lows, clears, jnp.stack([y, z, xh, c])]).astype(jnp.int32)

    def per_tile(values):
        rows = jnp.transpose(values.reshape(2, 4, 128), (1, 0, 2)).reshape(4, TILE)
        return jnp.concatenate([rows, rows], axis=1)

    bounds = jnp.stack([per_tile(index), per_tile(start)], axis=1)

    def kv_weight(across):
        which = y * 2 + (xl ^ across)
        parts = [lax.dynamic_slice_in_dim(w, which * 128, 128, 1) for w in (key_weight, value_weight)]
        return jnp.concatenate(parts, axis=1)

    kv_weights = barrier([kv_weight(0), kv_weight(1)])
    gain = norm_gain[None, :]
    pieces = [x[dy, dx].astype(f32) for dx in (0, 1) for dy in range(4)]
    rows = jnp.concatenate([(piece * gain).astype(bf16) for piece in pieces], axis=0)
    squares = jnp.stack([jnp.sum(piece * piece, axis=1) for piece in pieces])
    squares = squares + receive(squares, "c", 1)

    def half(rows, core):
        return lax.dynamic_slice_in_dim(rows, core * PART, PART, 0)

    def product(rows, weight):
        return jnp.dot(rows, weight, preferred_element_type=f32)

    away = half(rows, 1 - c)
    got_across = receive(product(away, kv_weights[1]).astype(bf16), "c", 1)
    got = receive(product(away, kv_weights[0]).astype(bf16), "c", 1)
    across = (product(half(rows, c), kv_weights[1]) + got_across.astype(f32)).astype(bf16)
    rows, across, squares = barrier((rows, across, squares))
    kv_far = receive(across, "xl", 1)
    kv_home = (product(half(rows, c), kv_weights[0]) + got.astype(f32)).astype(bf16)
    squares = squares + receive(squares, "xl", 1)
    scale = lax.rsqrt(squares.reshape(GROUP_ROWS, 1) / MODEL_WIDTH + norm_eps)
    total = (kv_home.astype(f32) + kv_far.astype(f32)) * half(scale, c)
    key, value = total[:, :HEAD_SIZE], total[:, HEAD_SIZE:]
    swapped_key = jnp.concatenate([key[:, HEAD_SIZE // 2 :], key[:, : HEAD_SIZE // 2]], axis=1)
    cos_half, sin_half = (lax.dynamic_index_in_dim(t, c, 0, keepdims=False) for t in (cosine, sine))
    key = key * cos_half + swapped_key * sin_half
    kv = jnp.stack([key.astype(bf16), value.astype(bf16)])
    rows, kv = barrier((rows, kv))
    mine = [kv] + [receive(kv, "z", step) for step in (1, 2, 3)]

    weights = weights.reshape(4, w_query.shape[0], w_query.shape[1])

    def query_weight(core, across):
        return lax.dynamic_index_in_dim(weights, (xl ^ across) * 2 + core, 0, keepdims=False)

    got_across = receive(product(rows, query_weight(1 - c, 1)).astype(bf16), "c", 1)
    got = receive(product(rows, query_weight(1 - c, 0)).astype(bf16), "c", 1)
    across = (product(rows, query_weight(c, 1)) + got_across.astype(f32)).astype(bf16)
    rows, across = barrier((rows, across))
    q_far = receive(across, "xl", 1)
    q_home = (product(rows, query_weight(c, 0)) + got.astype(f32)).astype(bf16)
    mine[1:], q_home, q_far = barrier((mine[1:], q_home, q_far))
    theirs = [receive(part, "c", 1) for part in mine]

    def all_heads(mixed, before):
        across = receive(mixed, "xl", 1)
        across, before = barrier((across, before))
        beside, diagonal = receive(mixed, "c", 1), receive(across, "c", 1)
        own = xl * 2 + c
        blocks = []
        for step in range(4):
            far = own ^ step
            near = jnp.where(far == 0, mixed, beside)
            blocks.append(jnp.where(far < 2, near, jnp.where(far == 2, across, diagonal)))
        return jnp.concatenate(blocks, axis=1), before

    y_first, seconds = {}, {}
    groups = ((2, 3), (1, 0))
    everything = (scalars, q_home, q_far, cosine, sine, scale, bounds, mine, theirs)
    mixed = [attention(tiles, *everything) for tiles in groups]
    for step, tiles in enumerate(groups):
        heads, before = all_heads(
            mixed[step].reshape(len(tiles) * TILE, WIDE), [y_first, seconds] if step else mixed[1]
        )
        if step:
            y_first, seconds = before
        else:
            mixed[1] = before
        second = jnp.dot(heads, w_out[:, columns:], preferred_element_type=f32).astype(bf16)
        second = second.reshape(len(tiles), 2, 128, columns)
        for i, dy in enumerate(tiles):
            seconds[dy] = second[i]
            y_first[dy] = jnp.dot(
                heads[i * TILE : (i + 1) * TILE], w_out[:, :columns], preferred_element_type=f32
            ).astype(bf16)
    xh_first = {}
    for tiles in groups:
        got = receive(jnp.stack([seconds[dy][1] for dy in tiles]), "xh", 1)
        for i, dy in enumerate(tiles):
            xh_first[dy] = (seconds[dy][0].astype(f32) + got[i].astype(f32)).astype(bf16)

    def sum_over_y(parts):
        total = parts[0].astype(f32)
        for dy in (2, 3, 1):
            total = total + receive(parts[dy], "y", -dy).astype(f32)
        return total

    first = sum_over_y(y_first)
    second = sum_over_y(xh_first)
    first = first[:128] + receive(first[128:].astype(bf16), "xh", 1).astype(f32)
    return jnp.concatenate([first, second], axis=1).astype(bf16)


def solution(mesh):
    fine = Mesh(mesh.devices.reshape(2, 2, 4, 4, 2), ("xl", "c", "y", "z", "xh"))
    blk, tensor = ("xl", "c"), ("y", "z", "xh")
    placed = (
        P(tensor, blk),
        P(blk),
        P(),
        P(blk, tensor),
        P(blk, None),
        P(blk, None),
        P(tensor, blk),
    )
    return jax.shard_map(
        shards, mesh=fine, in_specs=placed, out_specs=P(tensor, blk), check_vma=False
    )
```

```python
import functools
import math

import jax
import jax.numpy as jnp
from jax import lax
from jax.experimental import pallas as pl
from jax.experimental.pallas import tpu as pltpu
from jax.sharding import Mesh, PartitionSpec as P

MODEL_WIDTH = 8192
QUERY_HEADS = 64
KEY_VALUE_HEADS = 8
HEAD_SIZE = 128
TOKENS = 4096
SEGMENTS = 16
GROUP_ROWS = 1024
TILE = 256
PART = 512
WIDE = 2 * HEAD_SIZE

norm_eps = 1e-05
rope_base = 500000.0
MASKED = -1e30
VMEM = 60 * 2**20
LIGHT = pl.CostEstimate(flops=1, bytes_accessed=1, transcendentals=0)

f32 = jnp.float32
bf16 = jnp.bfloat16


def receive(value, axis, step):
    n = lax.axis_size(axis)
    return lax.ppermute(value, axis, [((i + step) % n, i) for i in range(n)])


def turn(u, cosine, sine):
    return u * cosine + pltpu.roll(u, HEAD_SIZE // 2, 1) * sine


def pick(tiles, i):
    chosen = jnp.int32(tiles[0])
    for at, tile in enumerate(tiles[1:], 1):
        chosen = jnp.where(i == at, jnp.int32(tile), chosen)
    return chosen


def attention_kernel(
    tiles, scalars, home0, home1, far0, far1, cosine, sine, scale0, scale1, bounds,
    m0, m1, m2, m3, t0, t1, t2, t3, out_ref, keys, values,
):
    place = pl.program_id(0)
    dy = pick(tiles, place)
    y, z, xh, c = scalars[8], scalars[9], scalars[10], scalars[11]

    @pl.when(place == 0)
    def _():
        for halves, dx in (((m0, m1, m2, m3), c), ((t0, t1, t2, t3), 1 - c)):
            for dz, ref in enumerate(halves):
                for i in range(4):
                    at = (lax.rem(y + i, 4) * 4 + lax.rem(z + dz, 4)) * TILE + (xh ^ dx) * 128
                    at = pl.ds(pl.multiple_of(at, 128), 128)
                    keys[at, :] = ref[0, i * 128 : (i + 1) * 128, :]
                    values[at, :] = ref[1, i * 128 : (i + 1) * 128, :]

    unit = f32(HEAD_SIZE ** (-0.5) * math.log2(math.e))
    turned = []
    for dx, (home, far, scale) in enumerate(((home0, far0, scale0), (home1, far1, scale1))):
        raw = (home[...].astype(f32) + far[...].astype(f32)) * (scale[...] * unit)
        for head in (0, 1):
            u = raw[:, head * HEAD_SIZE : (head + 1) * HEAD_SIZE]
            turned.append(turn(u, cosine[dx], sine[dx]).astype(bf16))
    q = jnp.concatenate([turned[0], turned[2], turned[1], turned[3]], axis=0)
    q_index = bounds[0, 0:1, :]
    q_start = bounds[0, 1:2, :]

    def step(masked, width, tile, carry):
        top, total, acc = carry
        first_key = tile * width
        at = pl.ds(pl.multiple_of(first_key, TILE), width)
        s = lax.dot_general(keys[at, :], q, (((1,), (1,)), ((), ())), preferred_element_type=f32)
        if masked:
            k_index = lax.broadcasted_iota(jnp.int32, (width, 1), 0) + first_key
            s = jnp.where((k_index <= q_index) & (k_index >= q_start), s, MASKED)
        new_top = jnp.maximum(top, jnp.max(s, axis=0, keepdims=True))
        p = jnp.exp2(s - new_top)
        decay = jnp.exp2(top - new_top)
        total = total * decay + jnp.sum(p, axis=0, keepdims=True)
        added = lax.dot_general(
            values[at, :], p.astype(bf16), (((0,), (0,)), ((), ())), preferred_element_type=f32
        )
        return new_top, total, acc * decay + added

    carry = (
        jnp.full((1, 2 * TILE), MASKED, f32),
        jnp.zeros((1, 2 * TILE), f32),
        jnp.zeros((HEAD_SIZE, 2 * TILE), f32),
    )
    last = lax.rem(y + dy, 4) * 4 + z
    first = scalars[dy]
    clear = jnp.minimum(scalars[4 + dy], last)
    big = 4
    big_first = (clear + big - 1) // big
    big_last = jnp.maximum(last // big, big_first)
    middle = jnp.minimum(big_first * big, last)
    one = functools.partial(step, False, TILE)
    carry = lax.fori_loop(first, clear, functools.partial(step, True, TILE), carry)
    carry = lax.fori_loop(clear, middle, one, carry)
    carry = lax.fori_loop(big_first, big_last, functools.partial(step, False, big * TILE), carry)
    carry = lax.fori_loop(jnp.maximum(big_last * big, middle), last, one, carry)
    top, total, acc = step(True, TILE, last, carry)
    result = (acc / total).T.astype(bf16)
    for head in (0, 1):
        for dx in (0, 1):
            at = head * TILE + dx * 128
            out_ref[0, dx, :, head * HEAD_SIZE : (head + 1) * HEAD_SIZE] = result[at : at + 128]


def attention(tiles, scalars, home, far, cosine, sine, scale, bounds, mine, theirs):
    def tile(i):
        return pick(tiles, i)

    half = pl.BlockSpec((2, PART, HEAD_SIZE), lambda i: (0, 0, 0))
    rows = [pl.BlockSpec((128, WIDE), lambda i, dx=dx: (4 * dx + tile(i), 0)) for dx in (0, 1)]
    angle = pl.BlockSpec((2, 128, HEAD_SIZE), lambda i: (0, tile(i), 0))
    column = [pl.BlockSpec((128, 1), lambda i, dx=dx: (4 * dx + tile(i), 0)) for dx in (0, 1)]
    return pl.pallas_call(
        functools.partial(attention_kernel, tiles),
        grid=(len(tiles),),
        in_specs=[pl.BlockSpec(memory_space=pltpu.SMEM)]
        + rows * 2
        + [angle] * 2
        + column
        + [pl.BlockSpec((1, 2, 2 * TILE), lambda i: (tile(i), 0, 0))]
        + [half] * 8,
        out_specs=pl.BlockSpec((1, 2, 128, WIDE), lambda i: (i, 0, 0, 0)),
        out_shape=jax.ShapeDtypeStruct((len(tiles), 2, 128, WIDE), bf16),
        scratch_shapes=[pltpu.VMEM((TOKENS, HEAD_SIZE), bf16)] * 2,
        compiler_params=pltpu.CompilerParams(vmem_limit_bytes=VMEM),
        cost_estimate=pl.CostEstimate(
            flops=len(tiles) * 10**9, bytes_accessed=2**22, transcendentals=len(tiles) * 10**6
        ),
    )(scalars, home, home, far, far, cosine, sine, scale, scale, bounds, *mine, *theirs)


def shards(tokens, norm_gain, segment_ids, w_query, key_weight, value_weight, w_output):
    xl, c, y, z, xh = (lax.axis_index(a) for a in ("xl", "c", "y", "z", "xh"))
    barrier = lax.optimization_barrier

    x = {(0, 0): tokens}
    x[1, 0] = receive(tokens, "y", 1)
    x[3, 0] = receive(tokens, "y", -1)
    x[0, 1] = receive(tokens, "xh", 1)
    x[2, 0] = receive(tokens, "y", 2)
    key_weight, value_weight, segment_ids, w_output, x[0, 1] = barrier(
        (key_weight, value_weight, segment_ids, w_output, x[0, 1])
    )
    x[1, 1] = receive(x[0, 1], "y", 1)
    x[3, 1] = receive(x[0, 1], "y", -1)
    x[2, 1] = receive(x[2, 0], "xh", 1)

    weights = lax.all_gather(w_query, "z", axis=0, tiled=True)
    w_out = lax.all_gather(w_output, "z", axis=0, tiled=True)
    columns = w_output.shape[1] // 2
    def relative(by_place):
        turned = lax.dynamic_slice_in_dim(jnp.concatenate([by_place, by_place], axis=0), y, 4, 0)
        swapped = jnp.where(xh == 0, turned, turned[:, ::-1])
        return jnp.transpose(swapped, (1, 0, 2)).reshape(2, PART)

    def own_rows(values):
        return relative(lax.dynamic_index_in_dim(values.reshape(4, 4, 2, 128), z, 1, keepdims=False))

    segments = own_rows(segment_ids)
    index = own_rows(jnp.arange(TOKENS, dtype=jnp.int32))
    ids = jnp.arange(SEGMENTS, dtype=jnp.int32)
    before = jnp.sum((segment_ids[None, :] < ids[:, None]).astype(jnp.int32), axis=1)
    start = jnp.sum(jnp.where(segments[None] == ids[:, None, None], before[:, None, None], 0), axis=0)
    places = (index - start).astype(f32)
    freqs = jnp.exp(jnp.arange(64, dtype=f32) * f32(-2.0 * math.log(rope_base) / HEAD_SIZE))
    angles = places[:, :, None] * freqs
    cosine, sine = jnp.cos(angles), jnp.sin(angles)
    cosine = jnp.concatenate([cosine, cosine], axis=2)
    sine = jnp.concatenate([-sine, sine], axis=2)
    by_tile = start.reshape(2, 4, 128)
    lows = jnp.min(by_tile, axis=(0, 2)) // TILE
    clears = (jnp.max(by_tile, axis=(0, 2)) + TILE - 1) // TILE
    scalars = jnp.concatenate([lows, clears, jnp.stack([y, z, xh, c])]).astype(jnp.int32)

    def per_tile(values):
        rows = jnp.transpose(values.reshape(2, 4, 128), (1, 0, 2)).reshape(4, TILE)
        return jnp.concatenate([rows, rows], axis=1)

    bounds = jnp.stack([per_tile(index), per_tile(start)], axis=1)

    def kv_weight(across):
        which = y * 2 + (xl ^ across)
        parts = [lax.dynamic_slice_in_dim(w, which * 128, 128, 1) for w in (key_weight, value_weight)]
        return jnp.concatenate(parts, axis=1)

    kv_weights = barrier([kv_weight(0), kv_weight(1)])
    gain = norm_gain[None, :]
    early = [x[dy, dx].astype(f32) for dx, dy in ((0, 0), (0, 1), (0, 2), (0, 3), (1, 0))]
    early = [jnp.sum(piece * piece, axis=1) for piece in early]
    x[1, 1], x[2, 1], x[3, 1], early = barrier((x[1, 1], x[2, 1], x[3, 1], early))
    pieces = [x[dy, dx].astype(f32) for dx in (0, 1) for dy in range(4)]
    rows = jnp.concatenate([(piece * gain).astype(bf16) for piece in pieces], axis=0)
    squares = early + [jnp.sum(piece * piece, axis=1) for piece in pieces[5:]]
    squares = jnp.stack(squares)
    squares = squares + receive(squares, "c", 1)

    def half(rows, core):
        return lax.dynamic_slice_in_dim(rows, core * PART, PART, 0)

    def product(rows, weight):
        return jnp.dot(rows, weight, preferred_element_type=f32)

    away = half(rows, 1 - c)
    got_across = receive(product(away, kv_weights[1]).astype(bf16), "c", 1)
    got = receive(product(away, kv_weights[0]).astype(bf16), "c", 1)
    across = (product(half(rows, c), kv_weights[1]) + got_across.astype(f32)).astype(bf16)
    rows, across, squares = barrier((rows, across, squares))
    kv_far = receive(across, "xl", 1)
    kv_home = (product(half(rows, c), kv_weights[0]) + got.astype(f32)).astype(bf16)
    squares = squares + receive(squares, "xl", 1)
    def query_weight(core, across):
        return lax.dynamic_index_in_dim(weights, (xl ^ across) * 2 + core, 0, keepdims=False)

    weights = weights.reshape(4, w_query.shape[0], w_query.shape[1])
    away = [product(rows, query_weight(1 - c, across)).astype(bf16) for across in (1, 0)]
    kv_far, away = barrier((kv_far, away))
    scale = lax.rsqrt(squares.reshape(GROUP_ROWS, 1) / MODEL_WIDTH + norm_eps)
    total = (kv_home.astype(f32) + kv_far.astype(f32)) * half(scale, c)
    key, value = total[:, :HEAD_SIZE], total[:, HEAD_SIZE:]
    swapped_key = jnp.concatenate([key[:, HEAD_SIZE // 2 :], key[:, : HEAD_SIZE // 2]], axis=1)
    cos_half, sin_half = (lax.dynamic_index_in_dim(t, c, 0, keepdims=False) for t in (cosine, sine))
    key = key * cos_half + swapped_key * sin_half
    kv = jnp.stack([key.astype(bf16), value.astype(bf16)])
    mine = [kv] + [receive(kv, "z", step) for step in (1, 2, 3)]

    got_across, got = (receive(part, "c", 1) for part in away)
    across = (product(rows, query_weight(c, 1)) + got_across.astype(f32)).astype(bf16)
    rows, across = barrier((rows, across))
    q_far = receive(across, "xl", 1)
    q_home = (product(rows, query_weight(c, 0)) + got.astype(f32)).astype(bf16)
    mine[1:], q_home, q_far, scalars, bounds, scale, cosine, sine = barrier(
        (mine[1:], q_home, q_far, scalars, bounds, scale, cosine, sine)
    )
    theirs = [receive(part, "c", 1) for part in mine]

    def all_heads(mixed, before):
        across = receive(mixed, "xl", 1)
        across, before = barrier((across, before))
        beside, diagonal = receive(mixed, "c", 1), receive(across, "c", 1)
        own = xl * 2 + c
        blocks = []
        for step in range(4):
            far = own ^ step
            near = jnp.where(far == 0, mixed, beside)
            blocks.append(jnp.where(far < 2, near, jnp.where(far == 2, across, diagonal)))
        return jnp.concatenate(blocks, axis=1), before

    y_first, seconds = {}, {}
    groups = ((2, 3), (1, 0))
    everything = (scalars, q_home, q_far, cosine, sine, scale, bounds, mine, theirs)
    mixed = [attention(tiles, *everything) for tiles in groups]
    for step, tiles in enumerate(groups):
        heads, before = all_heads(
            mixed[step].reshape(len(tiles) * TILE, WIDE), [y_first, seconds] if step else mixed[1]
        )
        if step:
            y_first, seconds = before
        else:
            mixed[1] = before
        second = jnp.dot(heads, w_out[:, columns:], preferred_element_type=f32).astype(bf16)
        second = second.reshape(len(tiles), 2, 128, columns)
        for i, dy in enumerate(tiles):
            seconds[dy] = second[i]
            y_first[dy] = jnp.dot(
                heads[i * TILE : (i + 1) * TILE], w_out[:, :columns], preferred_element_type=f32
            ).astype(bf16)
    def over_y(parts, dy):
        return receive(parts[dy], "y", -dy).astype(f32)

    xh_first, arrived = {}, {}
    for step, tiles in enumerate(groups):
        got = receive(jnp.stack([seconds[dy][1] for dy in tiles]), "xh", 1)
        if step == 1:
            got, arrived = barrier((got, arrived))
        for i, dy in enumerate(tiles):
            xh_first[dy] = (seconds[dy][0].astype(f32) + got[i].astype(f32)).astype(bf16)
            arrived[dy] = over_y(xh_first, dy) if dy else xh_first[0].astype(f32)

    first = y_first[0].astype(f32) + over_y(y_first, 2) + over_y(y_first, 3) + over_y(y_first, 1)
    second = arrived[0] + arrived[1] + arrived[2] + arrived[3]
    first = first[:128] + receive(first[128:].astype(bf16), "xh", 1).astype(f32)
    return jnp.concatenate([first, second], axis=1).astype(bf16)


def solution(mesh):
    fine = Mesh(mesh.devices.reshape(2, 2, 4, 4, 2), ("xl", "c", "y", "z", "xh"))
    blk, tensor = ("xl", "c"), ("y", "z", "xh")
    placed = (
        P(tensor, blk),
        P(blk),
        P(),
        P(blk, tensor),
        P(blk, None),
        P(blk, None),
        P(tensor, blk),
    )
    return jax.shard_map(
        shards, mesh=fine, in_specs=placed, out_specs=P(tensor, blk), check_vma=False
    )
```

```python
import functools
import math

import jax
import jax.numpy as jnp
from jax import lax
from jax.experimental import pallas as pl
from jax.experimental.pallas import tpu as pltpu
from jax.sharding import Mesh, PartitionSpec as P

MODEL_WIDTH = 8192
QUERY_HEADS = 64
KEY_VALUE_HEADS = 8
HEAD_SIZE = 128
TOKENS = 4096
SEGMENTS = 16
GROUP_ROWS = 1024
TILE = 256
PART = 512
WIDE = 2 * HEAD_SIZE

norm_eps = 1e-05
rope_base = 500000.0
MASKED = -1e30
VMEM = 60 * 2**20
LIGHT = pl.CostEstimate(flops=1, bytes_accessed=1, transcendentals=0)

f32 = jnp.float32
bf16 = jnp.bfloat16


def receive(value, axis, step):
    n = lax.axis_size(axis)
    return lax.ppermute(value, axis, [((i + step) % n, i) for i in range(n)])


def turn(u, cosine, sine):
    return u * cosine + pltpu.roll(u, HEAD_SIZE // 2, 1) * sine


def pick(tiles, i):
    chosen = jnp.int32(tiles[0])
    for at, tile in enumerate(tiles[1:], 1):
        chosen = jnp.where(i == at, jnp.int32(tile), chosen)
    return chosen


def attention_kernel(
    tiles, scalars, home0, home1, far0, far1, cosine, sine, scale0, scale1, bounds,
    m0, m1, m2, m3, t0, t1, t2, t3, out_ref, keys, values,
):
    place = pl.program_id(0)
    dy = pick(tiles, place)
    y, z, xh, c = scalars[8], scalars[9], scalars[10], scalars[11]

    @pl.when(place == 0)
    def _():
        for halves, dx in (((m0, m1, m2, m3), c), ((t0, t1, t2, t3), 1 - c)):
            for dz, ref in enumerate(halves):
                for i in range(4):
                    at = (lax.rem(y + i, 4) * 4 + lax.rem(z + dz, 4)) * TILE + (xh ^ dx) * 128
                    at = pl.ds(pl.multiple_of(at, 128), 128)
                    keys[at, :] = ref[0, i * 128 : (i + 1) * 128, :]
                    values[at, :] = ref[1, i * 128 : (i + 1) * 128, :]

    unit = f32(HEAD_SIZE ** (-0.5) * math.log2(math.e))
    turned = []
    for dx, (home, far, scale) in enumerate(((home0, far0, scale0), (home1, far1, scale1))):
        raw = (home[...].astype(f32) + far[...].astype(f32)) * (scale[...] * unit)
        for head in (0, 1):
            u = raw[:, head * HEAD_SIZE : (head + 1) * HEAD_SIZE]
            turned.append(turn(u, cosine[dx], sine[dx]).astype(bf16))
    q = jnp.concatenate([turned[0], turned[2], turned[1], turned[3]], axis=0)
    q_index = bounds[0, 0:1, :]
    q_start = bounds[0, 1:2, :]

    def step(masked, width, tile, carry):
        top, total, acc = carry
        first_key = tile * TILE
        at = pl.ds(pl.multiple_of(first_key, TILE), width)
        s = lax.dot_general(keys[at, :], q, (((1,), (1,)), ((), ())), preferred_element_type=f32)
        if masked:
            k_index = lax.broadcasted_iota(jnp.int32, (width, 1), 0) + first_key
            s = jnp.where((k_index <= q_index) & (k_index >= q_start), s, MASKED)
        new_top = jnp.maximum(top, jnp.max(s, axis=0, keepdims=True))
        p = jnp.exp2(s - new_top)
        decay = jnp.exp2(top - new_top)
        total = total * decay + jnp.sum(p, axis=0, keepdims=True)
        added = lax.dot_general(
            values[at, :], p.astype(bf16), (((0,), (0,)), ((), ())), preferred_element_type=f32
        )
        return new_top, total, acc * decay + added

    carry = (
        jnp.full((1, 2 * TILE), MASKED, f32),
        jnp.zeros((1, 2 * TILE), f32),
        jnp.zeros((HEAD_SIZE, 2 * TILE), f32),
    )
    last = lax.rem(y + dy, 4) * 4 + z
    first = scalars[dy]
    clear = jnp.minimum(scalars[4 + dy], last)
    count = last - clear
    carry = lax.fori_loop(first, clear, functools.partial(step, True, TILE), carry)
    carry = lax.fori_loop(
        0, count // 4, lambda i, carry: step(False, 4 * TILE, clear + 4 * i, carry), carry
    )
    rest = clear + count // 4 * 4
    carry = lax.fori_loop(
        0, lax.rem(count // 2, 2), lambda i, carry: step(False, 2 * TILE, rest, carry), carry
    )
    carry = lax.fori_loop(
        0, lax.rem(count, 2), lambda i, carry: step(False, TILE, last - 1, carry), carry
    )
    top, total, acc = step(True, TILE, last, carry)
    result = (acc / total).T.astype(bf16)
    for head in (0, 1):
        for dx in (0, 1):
            at = head * TILE + dx * 128
            out_ref[0, dx, :, head * HEAD_SIZE : (head + 1) * HEAD_SIZE] = result[at : at + 128]


def attention(tiles, scalars, home, far, cosine, sine, scale, bounds, mine, theirs):
    def tile(i):
        return pick(tiles, i)

    half = pl.BlockSpec((2, PART, HEAD_SIZE), lambda i: (0, 0, 0))
    rows = [pl.BlockSpec((128, WIDE), lambda i, dx=dx: (4 * dx + tile(i), 0)) for dx in (0, 1)]
    angle = pl.BlockSpec((2, 128, HEAD_SIZE), lambda i: (0, tile(i), 0))
    column = [pl.BlockSpec((128, 1), lambda i, dx=dx: (4 * dx + tile(i), 0)) for dx in (0, 1)]
    return pl.pallas_call(
        functools.partial(attention_kernel, tiles),
        grid=(len(tiles),),
        in_specs=[pl.BlockSpec(memory_space=pltpu.SMEM)]
        + rows * 2
        + [angle] * 2
        + column
        + [pl.BlockSpec((1, 2, 2 * TILE), lambda i: (tile(i), 0, 0))]
        + [half] * 8,
        out_specs=pl.BlockSpec((1, 2, 128, WIDE), lambda i: (i, 0, 0, 0)),
        out_shape=jax.ShapeDtypeStruct((len(tiles), 2, 128, WIDE), bf16),
        scratch_shapes=[pltpu.VMEM((TOKENS, HEAD_SIZE), bf16)] * 2,
        compiler_params=pltpu.CompilerParams(vmem_limit_bytes=VMEM),
        cost_estimate=pl.CostEstimate(
            flops=len(tiles) * 10**9, bytes_accessed=2**22, transcendentals=len(tiles) * 10**6
        ),
    )(scalars, home, home, far, far, cosine, sine, scale, scale, bounds, *mine, *theirs)


def shards(tokens, norm_gain, segment_ids, w_query, key_weight, value_weight, w_output):
    xl, c, y, z, xh = (lax.axis_index(a) for a in ("xl", "c", "y", "z", "xh"))
    barrier = lax.optimization_barrier

    x = {(0, 0): tokens}
    x[1, 0] = receive(tokens, "y", 1)
    x[3, 0] = receive(tokens, "y", -1)
    x[0, 1] = receive(tokens, "xh", 1)
    x[2, 0] = receive(tokens, "y", 2)
    key_weight, value_weight, segment_ids, w_output, x[0, 1] = barrier(
        (key_weight, value_weight, segment_ids, w_output, x[0, 1])
    )
    x[1, 1] = receive(x[0, 1], "y", 1)
    x[3, 1] = receive(x[0, 1], "y", -1)
    x[2, 1] = receive(x[2, 0], "xh", 1)

    weights = lax.all_gather(w_query, "z", axis=0, tiled=True)
    w_out = lax.all_gather(w_output, "z", axis=0, tiled=True)
    columns = w_output.shape[1] // 2
    def relative(by_place):
        turned = lax.dynamic_slice_in_dim(jnp.concatenate([by_place, by_place], axis=0), y, 4, 0)
        swapped = jnp.where(xh == 0, turned, turned[:, ::-1])
        return jnp.transpose(swapped, (1, 0, 2)).reshape(2, PART)

    def own_rows(values):
        return relative(lax.dynamic_index_in_dim(values.reshape(4, 4, 2, 128), z, 1, keepdims=False))

    segments = own_rows(segment_ids)
    index = own_rows(jnp.arange(TOKENS, dtype=jnp.int32))
    ids = jnp.arange(SEGMENTS, dtype=jnp.int32)
    before = jnp.sum((segment_ids[None, :] < ids[:, None]).astype(jnp.int32), axis=1)
    start = jnp.sum(jnp.where(segments[None] == ids[:, None, None], before[:, None, None], 0), axis=0)
    places = (index - start).astype(f32)
    freqs = jnp.exp(jnp.arange(64, dtype=f32) * f32(-2.0 * math.log(rope_base) / HEAD_SIZE))
    angles = places[:, :, None] * freqs
    cosine, sine = jnp.cos(angles), jnp.sin(angles)
    cosine = jnp.concatenate([cosine, cosine], axis=2)
    sine = jnp.concatenate([-sine, sine], axis=2)
    by_tile = start.reshape(2, 4, 128)
    lows = jnp.min(by_tile, axis=(0, 2)) // TILE
    clears = (jnp.max(by_tile, axis=(0, 2)) + TILE - 1) // TILE
    scalars = jnp.concatenate([lows, clears, jnp.stack([y, z, xh, c])]).astype(jnp.int32)

    def per_tile(values):
        rows = jnp.transpose(values.reshape(2, 4, 128), (1, 0, 2)).reshape(4, TILE)
        return jnp.concatenate([rows, rows], axis=1)

    bounds = jnp.stack([per_tile(index), per_tile(start)], axis=1)

    def kv_weight(across):
        which = y * 2 + (xl ^ across)
        parts = [lax.dynamic_slice_in_dim(w, which * 128, 128, 1) for w in (key_weight, value_weight)]
        return jnp.concatenate(parts, axis=1)

    kv_weights = barrier([kv_weight(0), kv_weight(1)])
    gain = norm_gain[None, :]
    early = [x[dy, dx].astype(f32) for dx, dy in ((0, 0), (0, 1), (0, 2), (0, 3), (1, 0))]
    early = [jnp.sum(piece * piece, axis=1) for piece in early]
    x[1, 1], x[2, 1], x[3, 1], early = barrier((x[1, 1], x[2, 1], x[3, 1], early))
    pieces = [x[dy, dx].astype(f32) for dx in (0, 1) for dy in range(4)]
    rows = jnp.concatenate([(piece * gain).astype(bf16) for piece in pieces], axis=0)
    squares = early + [jnp.sum(piece * piece, axis=1) for piece in pieces[5:]]
    squares = jnp.stack(squares)
    squares = squares + receive(squares, "c", 1)

    def half(rows, core):
        return lax.dynamic_slice_in_dim(rows, core * PART, PART, 0)

    def product(rows, weight):
        return jnp.dot(rows, weight, preferred_element_type=f32)

    away = half(rows, 1 - c)
    got_across = receive(product(away, kv_weights[1]).astype(bf16), "c", 1)
    got = receive(product(away, kv_weights[0]).astype(bf16), "c", 1)
    across = (product(half(rows, c), kv_weights[1]) + got_across.astype(f32)).astype(bf16)
    rows, across, squares = barrier((rows, across, squares))
    kv_far = receive(across, "xl", 1)
    kv_home = (product(half(rows, c), kv_weights[0]) + got.astype(f32)).astype(bf16)
    squares = squares + receive(squares, "xl", 1)
    def query_weight(core, across):
        return lax.dynamic_index_in_dim(weights, (xl ^ across) * 2 + core, 0, keepdims=False)

    weights = weights.reshape(4, w_query.shape[0], w_query.shape[1])
    away = [product(rows, query_weight(1 - c, across)).astype(bf16) for across in (1, 0)]
    kv_far, away = barrier((kv_far, away))
    scale = lax.rsqrt(squares.reshape(GROUP_ROWS, 1) / MODEL_WIDTH + norm_eps)
    total = (kv_home.astype(f32) + kv_far.astype(f32)) * half(scale, c)
    key, value = total[:, :HEAD_SIZE], total[:, HEAD_SIZE:]
    swapped_key = jnp.concatenate([key[:, HEAD_SIZE // 2 :], key[:, : HEAD_SIZE // 2]], axis=1)
    cos_half, sin_half = (lax.dynamic_index_in_dim(t, c, 0, keepdims=False) for t in (cosine, sine))
    key = key * cos_half + swapped_key * sin_half
    kv = jnp.stack([key.astype(bf16), value.astype(bf16)])
    mine = [kv] + [receive(kv, "z", step) for step in (1, 2, 3)]

    got_across, got = (receive(part, "c", 1) for part in away)
    across = (product(rows, query_weight(c, 1)) + got_across.astype(f32)).astype(bf16)
    rows, across = barrier((rows, across))
    q_far = receive(across, "xl", 1)
    q_home = (product(rows, query_weight(c, 0)) + got.astype(f32)).astype(bf16)
    mine[1:], q_home, q_far, scalars, bounds, scale, cosine, sine = barrier(
        (mine[1:], q_home, q_far, scalars, bounds, scale, cosine, sine)
    )
    theirs = [receive(part, "c", 1) for part in mine]

    def all_heads(mixed, before):
        across = receive(mixed, "xl", 1)
        across, before = barrier((across, before))
        beside, diagonal = receive(mixed, "c", 1), receive(across, "c", 1)
        own = xl * 2 + c
        blocks = []
        for step in range(4):
            far = own ^ step
            near = jnp.where(far == 0, mixed, beside)
            blocks.append(jnp.where(far < 2, near, jnp.where(far == 2, across, diagonal)))
        return jnp.concatenate(blocks, axis=1), before

    y_first, seconds = {}, {}
    groups = ((2, 3), (1, 0))
    everything = (scalars, q_home, q_far, cosine, sine, scale, bounds, mine, theirs)
    mixed = [attention(tiles, *everything) for tiles in groups]
    for step, tiles in enumerate(groups):
        heads, before = all_heads(
            mixed[step].reshape(len(tiles) * TILE, WIDE), [y_first, seconds] if step else mixed[1]
        )
        if step:
            y_first, seconds = before
        else:
            mixed[1] = before
        second = jnp.dot(heads, w_out[:, columns:], preferred_element_type=f32).astype(bf16)
        heads, second = barrier((heads, second))
        second = second.reshape(len(tiles), 2, 128, columns)
        for i, dy in enumerate(tiles):
            seconds[dy] = second[i]
            y_first[dy] = jnp.dot(
                heads[i * TILE : (i + 1) * TILE], w_out[:, :columns], preferred_element_type=f32
            ).astype(bf16)
    def over_y(parts, dy):
        return receive(parts[dy], "y", -dy).astype(f32)

    arrived = {}
    for tiles in ((2, 3), (1,), (0,)):
        got = receive(jnp.stack([seconds[dy][1] for dy in tiles]), "xh", 1)
        for i, dy in enumerate(tiles):
            both = seconds[dy][0].astype(f32) + got[i].astype(f32)
            arrived[dy] = over_y({dy: both.astype(bf16)}, dy) if dy else both

    first = y_first[0].astype(f32) + over_y(y_first, 2) + over_y(y_first, 3) + over_y(y_first, 1)
    second = arrived[0] + arrived[1] + arrived[2] + arrived[3]
    first = first[:128] + receive(first[128:].astype(bf16), "xh", 1).astype(f32)
    return jnp.concatenate([first, second], axis=1).astype(bf16)


def solution(mesh):
    fine = Mesh(mesh.devices.reshape(2, 2, 4, 4, 2), ("xl", "c", "y", "z", "xh"))
    blk, tensor = ("xl", "c"), ("y", "z", "xh")
    placed = (
        P(tensor, blk),
        P(blk),
        P(),
        P(blk, tensor),
        P(blk, None),
        P(blk, None),
        P(tensor, blk),
    )
    return jax.shard_map(
        shards, mesh=fine, in_specs=placed, out_specs=P(tensor, blk), check_vma=False
    )
```

```python
import functools
import math

import jax
import jax.numpy as jnp
from jax import lax
from jax.experimental import pallas as pl
from jax.experimental.pallas import tpu as pltpu
from jax.sharding import Mesh, PartitionSpec as P

MODEL_WIDTH = 8192
QUERY_HEADS = 64
KEY_VALUE_HEADS = 8
HEAD_SIZE = 128
TOKENS = 4096
SEGMENTS = 16
GROUP_ROWS = 1024
TILE = 256
PART = 512
WIDE = 2 * HEAD_SIZE

norm_eps = 1e-05
rope_base = 500000.0
MASKED = -1e30
VMEM = 60 * 2**20
LIGHT = pl.CostEstimate(flops=1, bytes_accessed=1, transcendentals=0)

f32 = jnp.float32
bf16 = jnp.bfloat16


def receive(value, axis, step):
    n = lax.axis_size(axis)
    return lax.ppermute(value, axis, [((i + step) % n, i) for i in range(n)])


def turn(u, cosine, sine):
    return u * cosine + pltpu.roll(u, HEAD_SIZE // 2, 1) * sine


def pick(tiles, i):
    chosen = jnp.int32(tiles[0])
    for at, tile in enumerate(tiles[1:], 1):
        chosen = jnp.where(i == at, jnp.int32(tile), chosen)
    return chosen


def attention_kernel(
    tiles, scalars, home0, home1, far0, far1, cosine, sine, scale0, scale1, bounds,
    m0, m1, m2, m3, t0, t1, t2, t3, out_ref, keys, values,
):
    place = pl.program_id(0)
    dy = pick(tiles, place)
    y, z, xh, c = scalars[8], scalars[9], scalars[10], scalars[11]

    @pl.when(place == 0)
    def _():
        for halves, dx in (((m0, m1, m2, m3), c), ((t0, t1, t2, t3), 1 - c)):
            for dz, ref in enumerate(halves):
                for i in range(4):
                    at = (lax.rem(y + i, 4) * 4 + lax.rem(z + dz, 4)) * TILE + (xh ^ dx) * 128
                    at = pl.ds(pl.multiple_of(at, 128), 128)
                    keys[at, :] = ref[0, i * 128 : (i + 1) * 128, :]
                    values[at, :] = ref[1, i * 128 : (i + 1) * 128, :]

    unit = f32(HEAD_SIZE ** (-0.5) * math.log2(math.e))
    turned = []
    for dx, (home, far, scale) in enumerate(((home0, far0, scale0), (home1, far1, scale1))):
        raw = (home[...].astype(f32) + far[...].astype(f32)) * (scale[...] * unit)
        for head in (0, 1):
            u = raw[:, head * HEAD_SIZE : (head + 1) * HEAD_SIZE]
            turned.append(turn(u, cosine[dx], sine[dx]).astype(bf16))
    q = jnp.concatenate([turned[0], turned[2], turned[1], turned[3]], axis=0)
    q_index = bounds[0, 0:1, :]
    q_start = bounds[0, 1:2, :]

    def step(masked, width, tile, carry):
        top, total, acc = carry
        first_key = tile * TILE
        at = pl.ds(pl.multiple_of(first_key, TILE), width)
        s = lax.dot_general(keys[at, :], q, (((1,), (1,)), ((), ())), preferred_element_type=f32)
        if masked:
            k_index = lax.broadcasted_iota(jnp.int32, (width, 1), 0) + first_key
            s = jnp.where((k_index <= q_index) & (k_index >= q_start), s, MASKED)
        new_top = jnp.maximum(top, jnp.max(s, axis=0, keepdims=True))
        p = jnp.exp2(s - new_top)
        decay = jnp.exp2(top - new_top)
        total = total * decay + jnp.sum(p, axis=0, keepdims=True)
        added = lax.dot_general(
            values[at, :], p.astype(bf16), (((0,), (0,)), ((), ())), preferred_element_type=f32
        )
        return new_top, total, acc * decay + added

    carry = (
        jnp.full((1, 2 * TILE), MASKED, f32),
        jnp.zeros((1, 2 * TILE), f32),
        jnp.zeros((HEAD_SIZE, 2 * TILE), f32),
    )
    last = lax.rem(y + dy, 4) * 4 + z
    first = scalars[dy]
    clear = jnp.minimum(scalars[4 + dy], last)
    count = last - clear
    carry = lax.fori_loop(first, clear, functools.partial(step, True, TILE), carry)
    carry = lax.fori_loop(
        0, count // 4, lambda i, carry: step(False, 4 * TILE, clear + 4 * i, carry), carry
    )
    rest = clear + count // 4 * 4
    carry = lax.fori_loop(
        0, lax.rem(count // 2, 2), lambda i, carry: step(False, 2 * TILE, rest, carry), carry
    )
    carry = lax.fori_loop(
        0, lax.rem(count, 2), lambda i, carry: step(False, TILE, last - 1, carry), carry
    )
    top, total, acc = step(True, TILE, last, carry)
    result = (acc / total).T.astype(bf16)
    for head in (0, 1):
        for dx in (0, 1):
            at = head * TILE + dx * 128
            out_ref[0, dx, :, head * HEAD_SIZE : (head + 1) * HEAD_SIZE] = result[at : at + 128]


def attention(tiles, scalars, home, far, cosine, sine, scale, bounds, mine, theirs):
    def tile(i):
        return pick(tiles, i)

    half = pl.BlockSpec((2, PART, HEAD_SIZE), lambda i: (0, 0, 0))
    rows = [pl.BlockSpec((128, WIDE), lambda i, dx=dx: (4 * dx + tile(i), 0)) for dx in (0, 1)]
    angle = pl.BlockSpec((2, 128, HEAD_SIZE), lambda i: (0, tile(i), 0))
    column = [pl.BlockSpec((128, 1), lambda i, dx=dx: (4 * dx + tile(i), 0)) for dx in (0, 1)]
    return pl.pallas_call(
        functools.partial(attention_kernel, tiles),
        grid=(len(tiles),),
        in_specs=[pl.BlockSpec(memory_space=pltpu.SMEM)]
        + rows * 2
        + [angle] * 2
        + column
        + [pl.BlockSpec((1, 2, 2 * TILE), lambda i: (tile(i), 0, 0))]
        + [half] * 8,
        out_specs=pl.BlockSpec((1, 2, 128, WIDE), lambda i: (i, 0, 0, 0)),
        out_shape=jax.ShapeDtypeStruct((len(tiles), 2, 128, WIDE), bf16),
        scratch_shapes=[pltpu.VMEM((TOKENS, HEAD_SIZE), bf16)] * 2,
        compiler_params=pltpu.CompilerParams(vmem_limit_bytes=VMEM),
        cost_estimate=pl.CostEstimate(
            flops=len(tiles) * 10**9, bytes_accessed=2**22, transcendentals=len(tiles) * 10**6
        ),
    )(scalars, home, home, far, far, cosine, sine, scale, scale, bounds, *mine, *theirs)


def shards(tokens, norm_gain, segment_ids, w_query, key_weight, value_weight, w_output):
    xl, c, y, z, xh = (lax.axis_index(a) for a in ("xl", "c", "y", "z", "xh"))
    barrier = lax.optimization_barrier

    x = {(0, 0): tokens}
    x[1, 0] = receive(tokens, "y", 1)
    x[3, 0] = receive(tokens, "y", -1)
    x[0, 1] = receive(tokens, "xh", 1)
    x[2, 0] = receive(tokens, "y", 2)
    key_weight, value_weight, segment_ids, w_output, x[0, 1] = barrier(
        (key_weight, value_weight, segment_ids, w_output, x[0, 1])
    )
    x[1, 1] = receive(x[0, 1], "y", 1)
    x[3, 1] = receive(x[0, 1], "y", -1)
    x[2, 1] = receive(x[2, 0], "xh", 1)

    weights = lax.all_gather(w_query, "z", axis=0, tiled=True)
    w_out = lax.all_gather(w_output, "z", axis=0, tiled=True)
    columns = w_output.shape[1] // 2
    def relative(by_place):
        turned = lax.dynamic_slice_in_dim(jnp.concatenate([by_place, by_place], axis=0), y, 4, 0)
        swapped = jnp.where(xh == 0, turned, turned[:, ::-1])
        return jnp.transpose(swapped, (1, 0, 2)).reshape(2, PART)

    def own_rows(values):
        return relative(lax.dynamic_index_in_dim(values.reshape(4, 4, 2, 128), z, 1, keepdims=False))

    segments = own_rows(segment_ids)
    index = own_rows(jnp.arange(TOKENS, dtype=jnp.int32))
    ids = jnp.arange(SEGMENTS, dtype=jnp.int32)
    before = jnp.sum((segment_ids[None, :] < ids[:, None]).astype(jnp.int32), axis=1)
    start = jnp.sum(jnp.where(segments[None] == ids[:, None, None], before[:, None, None], 0), axis=0)
    places = (index - start).astype(f32)
    freqs = jnp.exp(jnp.arange(64, dtype=f32) * f32(-2.0 * math.log(rope_base) / HEAD_SIZE))
    angles = places[:, :, None] * freqs
    cosine, sine = jnp.cos(angles), jnp.sin(angles)
    cosine = jnp.concatenate([cosine, cosine], axis=2)
    sine = jnp.concatenate([-sine, sine], axis=2)
    by_tile = start.reshape(2, 4, 128)
    lows = jnp.min(by_tile, axis=(0, 2)) // TILE
    clears = (jnp.max(by_tile, axis=(0, 2)) + TILE - 1) // TILE
    scalars = jnp.concatenate([lows, clears, jnp.stack([y, z, xh, c])]).astype(jnp.int32)

    def per_tile(values):
        rows = jnp.transpose(values.reshape(2, 4, 128), (1, 0, 2)).reshape(4, TILE)
        return jnp.concatenate([rows, rows], axis=1)

    bounds = jnp.stack([per_tile(index), per_tile(start)], axis=1)

    def kv_weight(across):
        which = y * 2 + (xl ^ across)
        parts = [lax.dynamic_slice_in_dim(w, which * 128, 128, 1) for w in (key_weight, value_weight)]
        return jnp.concatenate(parts, axis=1)

    kv_weights = barrier([kv_weight(0), kv_weight(1)])
    gain = norm_gain[None, :]
    early = [x[dy, dx].astype(f32) for dx, dy in ((0, 0), (0, 1), (0, 2), (0, 3), (1, 0))]
    early = [jnp.sum(piece * piece, axis=1) for piece in early]
    x[1, 1], x[2, 1], x[3, 1], early = barrier((x[1, 1], x[2, 1], x[3, 1], early))
    pieces = [x[dy, dx].astype(f32) for dx in (0, 1) for dy in range(4)]
    rows = jnp.concatenate([(piece * gain).astype(bf16) for piece in pieces], axis=0)
    squares = early + [jnp.sum(piece * piece, axis=1) for piece in pieces[5:]]
    squares = jnp.stack(squares)
    squares = squares + receive(squares, "c", 1)

    def half(rows, core):
        return lax.dynamic_slice_in_dim(rows, core * PART, PART, 0)

    def product(rows, weight):
        return jnp.dot(rows, weight, preferred_element_type=f32)

    away = half(rows, 1 - c)
    got_across = receive(product(away, kv_weights[1]).astype(bf16), "c", 1)
    got = receive(product(away, kv_weights[0]).astype(bf16), "c", 1)
    across = (product(half(rows, c), kv_weights[1]) + got_across.astype(f32)).astype(bf16)
    rows, across, squares = barrier((rows, across, squares))
    kv_far = receive(across, "xl", 1)
    kv_home = (product(half(rows, c), kv_weights[0]) + got.astype(f32)).astype(bf16)
    squares = squares + receive(squares, "xl", 1)
    def query_weight(core, across):
        return lax.dynamic_index_in_dim(weights, (xl ^ across) * 2 + core, 0, keepdims=False)

    weights = weights.reshape(4, w_query.shape[0], w_query.shape[1])
    away = [product(rows, query_weight(1 - c, across)).astype(bf16) for across in (1, 0)]
    kv_far, away = barrier((kv_far, away))
    scale = lax.rsqrt(squares.reshape(GROUP_ROWS, 1) / MODEL_WIDTH + norm_eps)
    total = (kv_home.astype(f32) + kv_far.astype(f32)) * half(scale, c)
    key, value = total[:, :HEAD_SIZE], total[:, HEAD_SIZE:]
    swapped_key = jnp.concatenate([key[:, HEAD_SIZE // 2 :], key[:, : HEAD_SIZE // 2]], axis=1)
    cos_half, sin_half = (lax.dynamic_index_in_dim(t, c, 0, keepdims=False) for t in (cosine, sine))
    key = key * cos_half + swapped_key * sin_half
    kv = jnp.stack([key.astype(bf16), value.astype(bf16)])
    mine = [kv] + [receive(kv, "z", step) for step in (1, 2, 3)]

    got_across, got = (receive(part, "c", 1) for part in away)
    across = (product(rows, query_weight(c, 1)) + got_across.astype(f32)).astype(bf16)
    rows, across = barrier((rows, across))
    q_far = receive(across, "xl", 1)
    q_home = (product(rows, query_weight(c, 0)) + got.astype(f32)).astype(bf16)
    mine[1:], q_home, q_far, scalars, bounds, scale, cosine, sine = barrier(
        (mine[1:], q_home, q_far, scalars, bounds, scale, cosine, sine)
    )
    theirs = [receive(part, "c", 1) for part in mine]

    def all_heads(mixed, before):
        across = receive(mixed, "xl", 1)
        across, before = barrier((across, before))
        beside, diagonal = receive(mixed, "c", 1), receive(across, "c", 1)
        own = xl * 2 + c
        blocks = []
        for step in range(4):
            far = own ^ step
            near = jnp.where(far == 0, mixed, beside)
            blocks.append(jnp.where(far < 2, near, jnp.where(far == 2, across, diagonal)))
        return jnp.concatenate(blocks, axis=1), before

    y_first, seconds = {}, {}
    groups = ((2, 3), (1, 0))
    everything = (scalars, q_home, q_far, cosine, sine, scale, bounds, mine, theirs)
    mixed = [attention(tiles, *everything) for tiles in groups]
    for step, tiles in enumerate(groups):
        heads, before = all_heads(
            mixed[step].reshape(len(tiles) * TILE, WIDE), [y_first, seconds] if step else mixed[1]
        )
        if step:
            y_first, seconds = before
        else:
            mixed[1] = before
        second = jnp.dot(heads, w_out[:, columns:], preferred_element_type=f32).astype(bf16)
        heads, second = barrier((heads, second))
        second = second.reshape(len(tiles), 2, 128, columns)
        for i, dy in enumerate(tiles):
            seconds[dy] = second[i]
            y_first[dy] = jnp.dot(
                heads[i * TILE : (i + 1) * TILE], w_out[:, :columns], preferred_element_type=f32
            ).astype(bf16)
    def over_y(parts, dy):
        return receive(parts[dy], "y", -dy).astype(f32)

    arrived = {}
    for tiles in ((2, 3), (1,), (0,)):
        got = receive(jnp.stack([seconds[dy][1] for dy in tiles]), "xh", 1)
        for i, dy in enumerate(tiles):
            both = seconds[dy][0].astype(f32) + got[i].astype(f32)
            arrived[dy] = over_y({dy: both.astype(bf16)}, dy) if dy else both

    leaving = receive(y_first[2][128:], "y", -2).astype(f32)
    staying = receive(y_first[2][:128], "y", -2).astype(f32)
    near = y_first[0].astype(f32) + over_y(y_first, 3) + over_y(y_first, 1)
    second = arrived[0] + arrived[1] + arrived[2] + arrived[3]
    last = receive((near[128:] + leaving).astype(bf16), "xh", 1).astype(f32)
    first = near[:128] + staying + last
    return jnp.concatenate([first, second], axis=1).astype(bf16)


def solution(mesh):
    fine = Mesh(mesh.devices.reshape(2, 2, 4, 4, 2), ("xl", "c", "y", "z", "xh"))
    blk, tensor = ("xl", "c"), ("y", "z", "xh")
    placed = (
        P(tensor, blk),
        P(blk),
        P(),
        P(blk, tensor),
        P(blk, None),
        P(blk, None),
        P(tensor, blk),
    )
    return jax.shard_map(
        shards, mesh=fine, in_specs=placed, out_specs=P(tensor, blk), check_vma=False
    )
```
